128 devices in a mesh: expert: 32 (over x, y, core), hidden: 4 (over z).
Axes of the slice: x: 4, y: 4, z: 4, core: 2. Of those that a mesh axis runs over, the one named last changes fastest.
Arguments:
- tokens: bfloat16 [8192, 2048], P('expert', 'hidden'), may hold values from -6 to 6
- cotangent: bfloat16 [8192, 2048], P('expert', 'hidden'), may hold values from -6 to 6
- zone_ids: int32 [8192, 2], P('expert'), may hold values from 0 to 127, all different within a row; in each aligned block of 256 rows (0 to 255, 256 to 511, ...) at most 8 rows name the same one
- gate_weights: float32 [8192, 2], P('expert'), may hold values from 0.1 to 1
- gate_proj: bfloat16 [128, 2048, 1024], P('expert', None, 'hidden'), may hold values from -0.125 to 0.125
- up_proj: bfloat16 [128, 2048, 1024], P('expert', None, 'hidden'), may hold values from -0.125 to 0.125
- down_proj: bfloat16 [128, 1024, 2048], P('expert', 'hidden'), may hold values from -0.1875 to 0.1875
Outputs:
- input_grad: bfloat16 [8192, 2048], P('expert', 'hidden')
- mix_grad: float32 [8192, 2], P('expert')
- gate_grad: bfloat16 [128, 2048, 1024], P('expert', None, 'hidden')
- up_grad: bfloat16 [128, 2048, 1024], P('expert', None, 'hidden')
- down_grad: bfloat16 [128, 1024, 2048], P('expert', 'hidden')
The draws below stay inside these ranges and needn't reach their ends.
Inputs may be any that keep to these rules, and one draw needn't show every extreme that they name: `zone_ids`: each row names two different experts. Among the rows of one device (aligned blocks of 256 rows) no expert is named more than 8 times, and in every draw some expert is named exactly 8 times in some block.
All inputs are finite; a program needn't handle non-finite values.
Results may differ from the reference program's by a relative error of at most 0.017.
Values may be sent and summed in bfloat16 or wider, within the bound.
No kernel may reach another device: no remote copies, remote signals or barrier semaphores. Data moves between devices by JAX's collectives and lax.ppermute only.
A program may use at most 128 MiB of HBM per device.

```python
import math
import jax
import jax.numpy as jnp
import numpy as np
from jax import lax

D = 2048
FF = 1024
TOK_DEV = 256
EXPERTS = 128
TOKENS = 8192
CAP = 8
N_EXPERT = 32
N_HIDDEN = 4


def block_scale(key, dims, pieces, smallest, high):
    loudness = 1.0
    for dim, blocks in pieces:
        heights = jax.random.uniform(jax.random.fold_in(jax.random.fold_in(key, 6), dim), (blocks,), jnp.float32, smallest / len(pieces), high / len(pieces))
        loudness = loudness * jnp.repeat(jnp.exp(heights), dims[dim] // blocks).reshape((-1,) + (1,) * (len(dims) - 1 - dim))
    return loudness


def routed_block(stream_key, own, number, rows, amount, top, most, skew):
    ranking = jax.random.permutation(stream_key, amount)
    heavy_load, usual = load_shares(amount, rows * top, most, skew, True), load_shares(amount, rows * top, most, skew, False)
    places = jnp.arange(amount)

    def named(lengths, rotation):
        used = int((lengths > 0).sum())
        fixed = max(1, used // 4)
        passed = fixed + (places - fixed + rotation * (used - fixed)) % max(1, amount - fixed)
        return jnp.zeros((amount,), jnp.int32).at[ranking[jnp.where(places < fixed, places, passed)]].set(jnp.asarray(lengths, jnp.int32))

    lengths = jnp.where(number % 4 == 0, named(heavy_load, number // 4), named(usual, number - number // 4 - 1))
    mixed = jax.random.permutation(jax.random.fold_in(own, 3), amount)
    giver, taker = mixed[0:amount // 2 * 2:2], mixed[1:amount // 2 * 2:2]
    margin = jnp.minimum(lengths[giver] - 1, most - lengths[taker]) // 2
    margin = jnp.where((giver == ranking[0]) | (taker == ranking[0]) | (lengths[taker] == 0), 0, jnp.maximum(margin, 0))
    passed = jax.random.randint(jax.random.fold_in(own, 4), (amount // 2,), 0, 1 << 20) % (margin + 1)
    lengths = lengths.at[giver].add(-passed).at[taker].add(passed)
    labels = jnp.searchsorted(jnp.cumsum(lengths), jnp.arange(rows * top), side="right").astype(jnp.int32)
    listing = labels.reshape(top, rows).T
    listing = listing[jax.random.permutation(jax.random.fold_in(own, 1), rows)]
    rotation = jax.random.randint(jax.random.fold_in(own, 2), (rows, 1), 0, top)
    return jnp.take_along_axis(listing, (jnp.arange(top)[None, :] + rotation) % top, axis=1)


def load_shares(number_of, total, bound, slope, full):
    portions = [(1 << 20) // math.isqrt(standing ** slope) + 1 for standing in range(1, number_of + 1)]
    largest = bound if full else min(bound, max(-(-total // number_of), total * portions[0] // sum(portions)))
    least = 1 if total - largest >= number_of - 1 else 0
    counts, surplus = [largest] + [least] * (number_of - 1), total - largest - least * (number_of - 1)
    while surplus > 0:
        candidates = [i for i in range(1, number_of) if counts[i] < largest] or [i for i in range(1, number_of) if counts[i] < bound]
        whole, budget = sum([portions[i] for i in candidates]), surplus
        for i in candidates:
            more = min(bound - counts[i], max(1, budget * portions[i] // whole), surplus)
            counts[i] = counts[i] + more
            surplus = surplus - more
    return np.array(counts)


def normal_values(rng, shape, width, reach, cuts=(), kind=jnp.bfloat16):
    drawn = width * jax.random.normal(rng, shape, jnp.float32)
    if cuts:
        drawn = drawn * block_scale(rng, shape, cuts, -0.22, 0.18)
    return jnp.clip(drawn, -reach, reach).astype(kind)


def setup_inputs(seed: int = 0) -> dict:
    key_of = jax.random.split(jax.random.key(seed), 8)
    tokens = normal_values(key_of[0], (TOKENS, D), 1.0, 6.0, ((0, 32), (1, 4)))
    cotangent = normal_values(key_of[1], (TOKENS, D), 1.0, 6.0, ((0, 32), (1, 4)))
    zone_ids_keys = jax.random.split(jax.random.fold_in(key_of[2], 1), TOKENS // TOK_DEV)
    zone_ids_turns = jax.random.permutation(jax.random.fold_in(key_of[2], 3), TOKENS // TOK_DEV)
    zone_ids = jax.vmap(lambda own, number: routed_block(jax.random.fold_in(key_of[2], 2), own, number, TOK_DEV, EXPERTS, 2, CAP, 2))(zone_ids_keys, zone_ids_turns).reshape((TOKENS, 2))
    gate_weights = jnp.clip(0.1 + 0.9 * jax.random.uniform(key_of[3], (TOKENS, 2), jnp.float32) ** block_scale(key_of[3], (TOKENS, 2), ((0, 32),), -0.2, 0.2), 0.1, 1.0)
    gate_proj = normal_values(key_of[4], (EXPERTS, D, FF), D ** -0.5, 0.125, ((0, 32), (2, 4)))
    up_proj = normal_values(key_of[5], (EXPERTS, D, FF), D ** -0.5, 0.125, ((0, 32), (2, 4)))
    down_proj = normal_values(key_of[6], (EXPERTS, FF, D), FF ** -0.5, 0.1875, ((0, 32), (1, 4)))
    return {"tokens": tokens, "cotangent": cotangent, "zone_ids": zone_ids, "gate_weights": gate_weights, "gate_proj": gate_proj, "up_proj": up_proj, "down_proj": down_proj}


def slot_table(block_ids, experts, cap):
    flat = block_ids.astype(jnp.int32)
    names = jnp.arange(experts, dtype=jnp.int32)
    onehot = (flat[:, None] == names[None, :]).astype(jnp.int32)
    earlier = jnp.cumsum(onehot, axis=0) - onehot
    rank = jnp.sum(earlier * onehot, axis=1).astype(jnp.int32)
    count = flat.shape[0]
    source_of = jnp.full((experts * cap,), -1, jnp.int32).at[flat * cap + rank].set(jnp.arange(count, dtype=jnp.int32))
    return rank, source_of


def one_expert(operands):
    x_rows, dy_rows, w_gate, w_up, w_down = operands
    rows = x_rows.shape[0]
    quarter = FF // N_HIDDEN
    g = jnp.dot(x_rows, w_gate, preferred_element_type=jnp.float32)
    u = jnp.dot(x_rows, w_up, preferred_element_type=jnp.float32)
    sig = jax.nn.sigmoid(g)
    silu_g = g * sig
    h = (silu_g * u).astype(jnp.bfloat16)
    h_parts = h.reshape(rows, N_HIDDEN, quarter).transpose(1, 0, 2).astype(jnp.float32)
    down_parts = w_down.reshape(N_HIDDEN, quarter, D).astype(jnp.float32)
    out_parts = jnp.einsum('qrf,qfd->qrd', h_parts, down_parts).astype(jnp.bfloat16)
    out_rows = jnp.sum(out_parts.astype(jnp.float32), axis=0).astype(jnp.bfloat16)
    down_grad = jnp.dot(h.T, dy_rows, preferred_element_type=jnp.float32).astype(jnp.bfloat16)
    dh = jnp.dot(dy_rows, w_down.T, preferred_element_type=jnp.float32)
    dg = (dh * u * sig * (1.0 + g * (1.0 - sig))).astype(jnp.bfloat16)
    du = (dh * silu_g).astype(jnp.bfloat16)
    gate_grad = jnp.dot(x_rows.T, dg, preferred_element_type=jnp.float32).astype(jnp.bfloat16)
    up_grad = jnp.dot(x_rows.T, du, preferred_element_type=jnp.float32).astype(jnp.bfloat16)
    dg_parts = dg.reshape(rows, N_HIDDEN, quarter).transpose(1, 0, 2).astype(jnp.float32)
    du_parts = du.reshape(rows, N_HIDDEN, quarter).transpose(1, 0, 2).astype(jnp.float32)
    gate_parts = w_gate.reshape(D, N_HIDDEN, quarter).transpose(1, 0, 2).astype(jnp.float32)
    up_parts = w_up.reshape(D, N_HIDDEN, quarter).transpose(1, 0, 2).astype(jnp.float32)
    dx_parts = jnp.einsum('qrf,qdf->qrd', dg_parts, gate_parts) + jnp.einsum('qrf,qdf->qrd', du_parts, up_parts)
    dx_rows = jnp.sum(dx_parts.astype(jnp.bfloat16).astype(jnp.float32), axis=0).astype(jnp.bfloat16)
    return out_rows, dx_rows, gate_grad, up_grad, down_grad


def reference(tokens, cotangent, zone_ids, gate_weights, gate_proj, up_proj, down_proj):
    pairs = 2 * TOK_DEV
    blocks = zone_ids.reshape(N_EXPERT, pairs)
    rank, source_of = jax.vmap(lambda ids: slot_table(ids, EXPERTS, CAP))(blocks)
    src = source_of.reshape(N_EXPERT, EXPERTS, CAP).transpose(1, 0, 2)
    valid = src >= 0
    safe = jnp.maximum(src, 0)
    base = jnp.arange(N_EXPERT, dtype=jnp.int32)[None, :, None]
    token_index = (base * TOK_DEV + safe // 2).reshape(EXPERTS, N_EXPERT * CAP)
    pair_index = (base * pairs + safe).reshape(EXPERTS, N_EXPERT * CAP)
    valid = valid.reshape(EXPERTS, N_EXPERT * CAP)
    weight = jnp.where(valid, gate_weights.reshape(-1)[pair_index], 0.0)
    x_slots = jnp.where(valid[..., None], tokens[token_index], jnp.zeros((), jnp.bfloat16))
    dy_slots = (cotangent[token_index].astype(jnp.float32) * weight[..., None]).astype(jnp.bfloat16)
    out_slots, dx_slots, gate_grad, up_grad, down_grad = lax.map(one_expert, (x_slots, dy_slots, gate_proj, up_proj, down_proj))
    expert_of = blocks
    block_of = jnp.arange(N_EXPERT, dtype=jnp.int32)[:, None]
    where = (expert_of * (N_EXPERT * CAP) + block_of * CAP + rank).reshape(-1)
    out_pairs = out_slots.reshape(EXPERTS * N_EXPERT * CAP, D)[where]
    dx_pairs = dx_slots.reshape(EXPERTS * N_EXPERT * CAP, D)[where]
    dy_pairs = jnp.repeat(cotangent, 2, axis=0)
    mix_grad = (jnp.sum(dy_pairs.astype(jnp.float32) * out_pairs.astype(jnp.float32), axis=1) * (D ** -0.5)).reshape(TOKENS, 2)
    input_grad = jnp.sum(dx_pairs.astype(jnp.float32).reshape(TOKENS, 2, D), axis=1).astype(jnp.bfloat16)
    return input_grad, mix_grad, gate_grad, up_grad, down_grad
```

```python
import jax
import jax.numpy as jnp
from jax import lax
from jax.experimental import pallas as pl
from jax.experimental.pallas import tpu as pltpu
from jax.sharding import PartitionSpec as P

D = 2048
SCALE = D ** (-0.5)
OWN = 32
NZ = 4
LOC = 4
CAP = 8
TOK = 256
QF = D // NZ
QH = 256
FA = 128
FB = QF - FA
RA = 384
RB = QF - RA
WA = QF + FA
WB = NZ * FB
WR = NZ * RB + 128
BF = jnp.bfloat16
F32 = jnp.float32
VMEM = 48 * 1024 * 1024


def dot(a, b, ca, cb):
    return lax.dot_general(a, b, (((ca,), (cb,)), ((), ())), preferred_element_type=F32)


def shift(x, d):
    return lax.ppermute(x, "hidden", [(i, (i + d) % NZ) for i in range(NZ)])


def params(**kw):
    return pltpu.CompilerParams(vmem_limit_bytes=VMEM, **kw)


def slots_of(dest, base, rows):
    slot = lax.broadcasted_iota(jnp.int32, (rows, TOK), 0) + base
    return slot == dest[0:1, :], slot == dest[1:2, :]


def route_first(zones, weights, tokens, cot, pay, dest_out, dest):
    step = pl.program_id(0)

    @pl.when(step == 0)
    def _():
        expert = lax.broadcasted_iota(jnp.int32, (OWN * LOC, TOK), 0)
        hit0 = expert == zones[0:1, :]
        hit1 = expert == zones[1:2, :]
        both = jnp.where(hit0 | hit1, 1.0, 0.0).astype(BF)
        earlier = lax.broadcasted_iota(jnp.int32, (TOK, TOK), 0) < lax.broadcasted_iota(
            jnp.int32, (TOK, TOK), 1
        )
        count = dot(both, jnp.where(earlier, 1.0, 0.0).astype(BF), 1, 0)
        rank0 = jnp.sum(jnp.where(hit0, count, 0.0), axis=0, keepdims=True)
        rank1 = jnp.sum(jnp.where(hit1, count, 0.0), axis=0, keepdims=True)
        dest[0:1, :] = zones[0:1, :] * CAP + rank0.astype(jnp.int32)
        dest[1:2, :] = zones[1:2, :] * CAP + rank1.astype(jnp.int32)
        dest_out[...] = dest[...]

    at0, at1 = slots_of(dest, step * 256, 256)
    pick = jnp.where(at0 | at1, 1.0, 0.0).astype(BF)
    w = jnp.sum(
        jnp.where(at0, weights[0:1, :], 0.0) + jnp.where(at1, weights[1:2, :], 0.0),
        axis=1,
        keepdims=True,
    )
    x = dot(pick, tokens[...], 1, 0).astype(BF)
    pay[:, :, :QF] = x.reshape(8, 32, QF)
    dy = (dot(pick, cot[:, :FA], 1, 0) * w).astype(BF)
    pay[:, :, QF:] = dy.reshape(8, 32, FA)


def route_rest(dest, weights, c0, c1, c2, c3, pay):
    at0, at1 = slots_of(dest, pl.program_id(0) * 256, 256)
    pick = jnp.where(at0 | at1, 1.0, 0.0).astype(BF)
    w = jnp.sum(
        jnp.where(at0, weights[0:1, :], 0.0) + jnp.where(at1, weights[1:2, :], 0.0),
        axis=1,
        keepdims=True,
    )
    for off, c in enumerate((c0, c1, c2, c3)):
        dy = (dot(pick, c[:, FA:], 1, 0) * w).astype(BF)
        pay[:, :, off * FB : (off + 1) * FB] = dy.reshape(8, 32, FB)


def merged(v):
    n, r, f = v.shape
    return v.astype(F32).reshape(n * r, f).astype(BF)


def assemble(z, own, left, right, far_a, far_b, rest, xs, dys):
    for off, parts in ((0, (own,)), (3, (left,)), (1, (right,)), (2, (far_a, far_b))):
        q = lax.rem(z + off, NZ)
        row = 0
        for part in parts:
            n = part.shape[0] * CAP
            xs[q, row : row + n, :] = merged(part[:, 0, :, :QF])
            dys[q, row : row + n, :FA] = merged(part[:, 0, :, QF:])
            row += n
        dys[q, :, FA:] = merged(rest[:, 0, :, off * FB : (off + 1) * FB])


def parted(v):
    return v.reshape(v.shape[0] // CAP, CAP, v.shape[1]).astype(BF)


def middle(
    z_ref, own, left, right, far_a, far_b, rest, wg, wu, wd,
    o0, o1t, o1b, o2t, o2b, o3t, o3b, part_out, h_out, dg_out, du_out, xs, dys,
):
    z = z_ref[0]
    assemble(z, own, left, right, far_a, far_b, rest, xs, dys)
    g = u = dh = 0.0
    for q in range(NZ):
        rows = slice(q * QF, (q + 1) * QF)
        g = g + dot(xs[q], wg[0, rows, :], 1, 0)
        u = u + dot(xs[q], wu[0, rows, :], 1, 0)
        dh = dh + dot(dys[q], wd[0, :, rows], 1, 1)
    sig = jax.nn.sigmoid(g)
    silu = g * sig
    h = (silu * u).astype(BF)
    dg = (dh * u * sig * (1.0 + g * (1.0 - sig))).astype(BF)
    du = (dh * silu).astype(BF)
    h_out[0] = h
    dg_out[0] = dg
    du_out[0] = du
    mix = jnp.sum(h.astype(F32) * dh, axis=1, keepdims=True)
    high = mix.astype(BF).astype(F32)
    lane = lax.broadcasted_iota(jnp.int32, (OWN * CAP, 128), 1)
    mix = jnp.where(lane == 0, high, jnp.where(lane == 1, mix - high, 0.0))
    part_out[:, 0, :, NZ * RB :] = parted(mix)
    for off, outs in ((2, (o2t, o2b)), (1, (o1t, o1b)), (3, (o3t, o3b)), (0, (o0,))):
        rows = pl.ds(pl.multiple_of(lax.rem(z + off, NZ) * QF, QF), QF)
        dx = dot(dg, wg[0, rows, :], 1, 1) + dot(du, wu[0, rows, :], 1, 1)
        row = 0
        for out in outs:
            n = out.shape[0] * CAP
            out[:, 0] = parted(dx[row : row + n, :RA])
            row += n
        part_out[:, 0, :, off * RB : (off + 1) * RB] = parted(dx[:, RA:])


def grads(
    z_ref, own, left, right, far_a, far_b, rest, h, dg, du,
    gate_out, up_out, down_out, xs, dys,
):
    assemble(z_ref[0], own, left, right, far_a, far_b, rest, xs, dys)
    for q in range(NZ):
        rows = slice(q * QF, (q + 1) * QF)
        gate_out[0, rows, :] = dot(xs[q], dg[0], 0, 0).astype(BF)
        up_out[0, rows, :] = dot(xs[q], du[0], 0, 0).astype(BF)
        down_out[0, :, rows] = dot(h[0], dys[q], 0, 0).astype(BF)


def pick_pairs(dest, back, y0, y1, y2, y3, mix_out):
    at0, at1 = slots_of(dest, 0, OWN * LOC * CAP)
    one0 = jnp.where(at0, 1.0, 0.0).astype(BF)
    one1 = jnp.where(at1, 1.0, 0.0).astype(BF)
    y = dot(one0 + one1, back[:, : NZ * RB], 0, 0).astype(BF)
    for off, out in enumerate((y0, y1, y2, y3)):
        out[...] = y[:, off * RB : (off + 1) * RB]
    m0 = dot(back[:, NZ * RB :], one0, 0, 0)
    m1 = dot(back[:, NZ * RB :], one1, 0, 0)
    mix_out[...] = jnp.zeros_like(mix_out)
    mix_out[0:1, :] = m0[0:1, :] + m0[1:2, :]
    mix_out[1:2, :] = m1[0:1, :] + m1[1:2, :]


def finish(dest, weights, back, y0, y1, y2, y3, m0, m1, m2, m3, grad_out, mix_out):
    at0, at1 = slots_of(dest, 0, OWN * LOC * CAP)
    pick = jnp.where(at0 | at1, 1.0, 0.0).astype(BF)
    grad_out[:, :RA] = dot(pick, back[...], 0, 0).astype(BF)
    y = (y0[...].astype(F32) + y2[...].astype(F32)) + (y1[...].astype(F32) + y3[...].astype(F32))
    grad_out[:, RA:] = y.astype(BF)
    total = (m0[...] + m2[...]) + (m1[...] + m3[...])
    mix_out[...] = total[0:2, :] * SCALE / weights[...]


def shape(dims, dtype=BF):
    return jax.ShapeDtypeStruct(dims, dtype)


def cost(flops, size):
    return pl.CostEstimate(flops=int(flops), bytes_accessed=int(size), transcendentals=0)


def whole(dims):
    return pl.BlockSpec(dims, lambda i: (0,) * len(dims))


def by_expert(n, width):
    return pl.BlockSpec((n, 1, CAP, width), lambda e: (0, e, 0, 0))


def leading(*dims):
    return pl.BlockSpec((1,) + dims, lambda e: (e,) + (0,) * len(dims))


def on_device(tokens, cotangent, zone_ids, gate_weights, gate_proj, up_proj, down_proj):
    z = lax.axis_index("hidden").astype(jnp.int32).reshape(1)
    zones, weights = zone_ids.T, gate_weights.T
    cots = (cotangent, shift(cotangent, -1), shift(cotangent, 2), shift(cotangent, 1))

    pay, dest = pl.pallas_call(
        route_first,
        grid=(4,),
        in_specs=[whole((2, TOK)), whole((2, TOK)), whole((TOK, QF)), whole((TOK, QF))],
        out_specs=[pl.BlockSpec((8, 32, WA), lambda i: (i, 0, 0)), whole((2, TOK))],
        out_shape=[shape((OWN, 32, WA)), shape((2, TOK), jnp.int32)],
        scratch_shapes=[pltpu.VMEM((2, TOK), jnp.int32)],
        compiler_params=params(),
        cost_estimate=cost(5e8, 4e6),
        name="route_first",
    )(zones, weights, tokens, cotangent)
    got = lax.all_to_all(pay, "expert", split_axis=0, concat_axis=0, tiled=True)

    pay_rest = pl.pallas_call(
        route_rest,
        grid=(4,),
        in_specs=[whole((2, TOK)), whole((2, TOK))] + [whole((TOK, QF))] * 4,
        out_specs=pl.BlockSpec((8, 32, WB), lambda i: (i, 0, 0)),
        out_shape=shape((OWN, 32, WB)),
        compiler_params=params(),
        cost_estimate=cost(8e8, 6e6),
        name="route_rest",
    )(dest, weights, *cots)
    rest = lax.all_to_all(pay_rest, "expert", split_axis=0, concat_axis=0, tiled=True)
    rest = rest.reshape(OWN, LOC, CAP, WB)

    half = OWN // 2
    got = got.reshape(OWN, LOC, CAP, WA)
    top, bot = got[:half], got[half:]
    left_t = shift(top, 1)
    right_b = shift(bot, -1)
    left_b = shift(bot, 1)
    right_t = shift(top, -1)
    far_t = shift(left_t, 1)
    far_b = shift(right_b, -1)
    left = jnp.concatenate([left_t, left_b], axis=0)
    right = jnp.concatenate([right_t, right_b], axis=0)

    act_in = (z, got, left, right, far_t, far_b, rest)
    act_specs = [
        pl.BlockSpec(memory_space=pltpu.SMEM),
        by_expert(OWN, WA), by_expert(OWN, WA), by_expert(OWN, WA),
        by_expert(half, WA), by_expert(half, WA), by_expert(OWN, WB),
    ]
    act_scratch = [pltpu.VMEM((NZ, OWN * CAP, QF), BF), pltpu.VMEM((NZ, OWN * CAP, QF), BF)]
    hid = shape((LOC, OWN * CAP, QH))
    whole_part = shape((OWN, LOC, CAP, RA))
    half_part = shape((half, LOC, CAP, RA))
    o0, o1t, o1b, o2t, o2b, o3t, o3b, part, h, dg, du = pl.pallas_call(
        middle,
        grid=(LOC,),
        in_specs=act_specs + [leading(D, QH), leading(D, QH), leading(QH, D)],
        out_specs=[by_expert(OWN, RA)] + [by_expert(half, RA)] * 6 + [by_expert(OWN, WR)]
        + [leading(OWN * CAP, QH)] * 3,
        out_shape=[whole_part] + [half_part] * 6 + [shape((OWN, LOC, CAP, WR)), hid, hid, hid],
        scratch_shapes=act_scratch,
        compiler_params=params(),
        cost_estimate=cost(5.4e9, 27e6),
        name="middle",
    )(*act_in, gate_proj, up_proj, down_proj)

    relay_t = shift(o2t, 1)
    relay_b = shift(o2b, -1)
    from_l_b = shift(o1b, 1)
    from_r_t = shift(o3t, -1)
    from_l_t = shift((o1t.astype(F32) + relay_t.astype(F32)).astype(BF), 1)
    from_r_b = shift((o3b.astype(F32) + relay_b.astype(F32)).astype(BF), -1)

    part_back = lax.all_to_all(
        part.reshape(OWN, 32, WR), "expert", split_axis=0, concat_axis=0, tiled=True
    ).reshape(OWN * 32, WR)

    sum_t = o0[:half].astype(F32) + from_l_t.astype(F32) + from_r_t.astype(F32)
    sum_b = o0[half:].astype(F32) + from_l_b.astype(F32) + from_r_b.astype(F32)
    sums = jnp.concatenate([sum_t.astype(BF), sum_b.astype(BF)], axis=0)
    back = lax.all_to_all(
        sums.reshape(OWN, 32, RA), "expert", split_axis=0, concat_axis=0, tiled=True
    ).reshape(OWN * 32, RA)

    y_shape = shape((TOK, RB))
    y0, y1, y2, y3, mix = pl.pallas_call(
        pick_pairs,
        out_shape=[y_shape] * 4 + [shape((8, TOK), F32)],
        compiler_params=params(),
        cost_estimate=cost(4e8, 3e6),
        name="pick_pairs",
    )(dest, part_back)
    ys = (y0, shift(y1, 1), shift(y2, 2), shift(y3, -1))
    mixes = (mix, shift(mix, 1), shift(mix, 2), shift(mix, -1))

    gate_grad, up_grad, down_grad = pl.pallas_call(
        grads,
        grid=(LOC,),
        in_specs=act_specs + [leading(OWN * CAP, QH)] * 3,
        out_specs=[leading(D, QH), leading(D, QH), leading(QH, D)],
        out_shape=[shape((LOC, D, QH)), shape((LOC, D, QH)), shape((LOC, QH, D))],
        scratch_shapes=act_scratch,
        compiler_params=params(),
        cost_estimate=cost(3.3e9, 30e6),
        name="grads",
    )(*act_in, h, dg, du)

    input_grad, mix_t = pl.pallas_call(
        finish,
        out_shape=[shape((TOK, QF)), shape((2, TOK), F32)],
        compiler_params=params(),
        cost_estimate=cost(4e8, 3e6),
        name="finish",
    )(dest, weights, back, *ys, *mixes)
    return (input_grad, mix_t.T, gate_grad, up_grad, down_grad)


def solution(mesh):
    return jax.shard_map(
        on_device,
        mesh=mesh,
        in_specs=(
            P("expert", "hidden"),
            P("expert", "hidden"),
            P("expert", None),
            P("expert", None),
            P("expert", None, "hidden"),
            P("expert", None, "hidden"),
            P("expert", "hidden", None),
        ),
        out_specs=(
            P("expert", "hidden"),
            P("expert", None),
            P("expert", None, "hidden"),
            P("expert", None, "hidden"),
            P("expert", "hidden", None),
        ),
        check_vma=False,
    )
```

```python
import jax
import jax.numpy as jnp
from jax import lax
from jax.experimental import pallas as pl
from jax.experimental.pallas import tpu as pltpu
from jax.sharding import PartitionSpec as P

D = 2048
SCALE = D ** (-0.5)
OWN = 32
NZ = 4
LOC = 4
CAP = 8
TOK = 256
QF = D // NZ
QH = 256
RA = 384
RB = QF - RA
WR = NZ * RB + 128
BF = jnp.bfloat16
F32 = jnp.float32
VMEM = 63 * 1024 * 1024


def dot(a, b, ca, cb):
    return lax.dot_general(a, b, (((ca,), (cb,)), ((), ())), preferred_element_type=F32)


def shift(x, d):
    return lax.ppermute(x, "hidden", [(i, (i + d) % NZ) for i in range(NZ)])


def params(**kw):
    return pltpu.CompilerParams(vmem_limit_bytes=VMEM, **kw)


def slots_of(dest, base, rows):
    slot = lax.broadcasted_iota(jnp.int32, (rows, TOK), 0) + base
    return slot == dest[0:1, :], slot == dest[1:2, :]


def route_first(zones, tokens, pay, dest_out, dest):
    step = pl.program_id(0)

    @pl.when(step == 0)
    def _():
        expert = lax.broadcasted_iota(jnp.int32, (OWN * LOC, TOK), 0)
        hit0 = expert == zones[0:1, :]
        hit1 = expert == zones[1:2, :]
        both = jnp.where(hit0 | hit1, 1.0, 0.0).astype(BF)
        earlier = lax.broadcasted_iota(jnp.int32, (TOK, TOK), 0) < lax.broadcasted_iota(
            jnp.int32, (TOK, TOK), 1
        )
        count = dot(both, jnp.where(earlier, 1.0, 0.0).astype(BF), 1, 0)
        rank0 = jnp.sum(jnp.where(hit0, count, 0.0), axis=0, keepdims=True)
        rank1 = jnp.sum(jnp.where(hit1, count, 0.0), axis=0, keepdims=True)
        dest[0:1, :] = zones[0:1, :] * CAP + rank0.astype(jnp.int32)
        dest[1:2, :] = zones[1:2, :] * CAP + rank1.astype(jnp.int32)
        dest_out[...] = dest[...]

    at0, at1 = slots_of(dest, step * 256, 256)
    pick = jnp.where(at0 | at1, 1.0, 0.0).astype(BF)
    pay[...] = dot(pick, tokens[...], 1, 0).astype(BF).reshape(8, 32, QF)


def route_rest(z_ref, dest, weights, c0, c1, c2, c3, pay):
    at0, at1 = slots_of(dest, pl.program_id(0) * 256, 256)
    pick = jnp.where(at0 | at1, 1.0, 0.0).astype(BF)
    w = jnp.sum(
        jnp.where(at0, weights[0:1, :], 0.0) + jnp.where(at1, weights[1:2, :], 0.0),
        axis=1,
        keepdims=True,
    )
    for off, c in enumerate((c0, c1, c2, c3)):
        dy = (dot(pick, c[...], 1, 0) * w).astype(BF)
        q = lax.rem(z_ref[0] + off, NZ)
        pay[:, :, pl.ds(pl.multiple_of(q * QF, QF), QF)] = dy.reshape(8, 32, QF)


def merged(v):
    n, r, f = v.shape
    return v.astype(F32).reshape(n * r, f).astype(BF)


def parted(v):
    return v.reshape(v.shape[0] // CAP, CAP, v.shape[1]).astype(BF)


def gates(
    z_ref, own, left_a, left_b, right_a, right_b, far_a, far_b, wg, wu,
    x_out, h_out, silu_out, slope_out, xs,
):
    pieces = ((0, (own,)), (3, (left_a, left_b)), (1, (right_a, right_b)), (2, (far_a, far_b)))
    for off, parts in pieces:
        q = lax.rem(z_ref[0] + off, NZ)
        row = 0
        for part in parts:
            n = part.shape[0] * CAP
            xs[q, row : row + n, :] = merged(part[:, 0])
            row += n
    g = u = 0.0
    for q in range(NZ):
        rows = slice(q * QF, (q + 1) * QF)
        x_out[0, :, rows] = xs[q]
        g = g + dot(xs[q], wg[0, rows, :], 1, 0)
        u = u + dot(xs[q], wu[0, rows, :], 1, 0)
    sig = jax.nn.sigmoid(g)
    silu = g * sig
    h_out[0] = (silu * u).astype(BF)
    silu_out[0] = silu
    slope_out[0] = u * sig * (1.0 + g * (1.0 - sig))


def middle(
    z_ref, rest, h_in, silu, slope, wg, wu, wd,
    o0, o1t, o1b, o2t, o2b, o3t, o3b, part_out, dg_out, du_out,
):
    z = z_ref[0]
    h = h_in[0]
    dh = dot(merged(rest[:, 0]), wd[0], 1, 1)
    dg = (dh * slope[0]).astype(BF)
    du = (dh * silu[0]).astype(BF)
    dg_out[0] = dg
    du_out[0] = du
    mix = jnp.sum(h.astype(F32) * dh, axis=1, keepdims=True)
    high = mix.astype(BF).astype(F32)
    lane = lax.broadcasted_iota(jnp.int32, (OWN * CAP, 128), 1)
    mix = jnp.where(lane == 0, high, jnp.where(lane == 1, mix - high, 0.0))
    part_out[:, 0, :, NZ * RB :] = parted(mix)
    for off, outs in ((2, (o2t, o2b)), (1, (o1t, o1b)), (3, (o3t, o3b)), (0, (o0,))):
        rows = pl.ds(pl.multiple_of(lax.rem(z + off, NZ) * QF, QF), QF)
        dx = dot(dg, wg[0, rows, :], 1, 1) + dot(du, wu[0, rows, :], 1, 1)
        row = 0
        for out in outs:
            n = out.shape[0] * CAP
            out[:, 0] = parted(dx[row : row + n, :RA])
            row += n
        part_out[:, 0, :, off * RB : (off + 1) * RB] = parted(dx[:, RA:])


def grads(x, rest, h, dg, du, gate_out, up_out, down_out):
    gate_out[0] = dot(x[0], dg[0], 0, 0).astype(BF)
    up_out[0] = dot(x[0], du[0], 0, 0).astype(BF)
    down_out[0] = dot(h[0], merged(rest[:, 0]), 0, 0).astype(BF)


def pick_pairs(dest, back, y0, y1, y2, y3):
    at0, at1 = slots_of(dest, 0, OWN * LOC * CAP)
    one0 = jnp.where(at0, 1.0, 0.0).astype(BF)
    one1 = jnp.where(at1, 1.0, 0.0).astype(BF)
    y = dot(one0 + one1, back[:, : NZ * RB], 0, 0).astype(BF)
    m0 = dot(back[:, NZ * RB :], one0, 0, 0)
    m1 = dot(back[:, NZ * RB :], one1, 0, 0)
    rows = [m[:8, c : c + RB] for m in (m0, m1) for c in range(0, TOK, RB)]
    mix = jnp.concatenate(rows, axis=0).astype(BF)
    for off, out in enumerate((y0, y1, y2, y3)):
        out[:TOK, :] = y[:, off * RB : (off + 1) * RB]
        out[TOK:, :] = mix


def finish(dest, weights, back, y0, y1, y2, y3, grad_out, mix_out):
    at0, at1 = slots_of(dest, 0, OWN * LOC * CAP)
    pick = jnp.where(at0 | at1, 1.0, 0.0).astype(BF)
    grad_out[:, :RA] = dot(pick, back[...], 0, 0).astype(BF)
    y = (y0[...].astype(F32) + y2[...].astype(F32)) + (y1[...].astype(F32) + y3[...].astype(F32))
    grad_out[:, RA:] = y[:TOK].astype(BF)
    for k in range(2):
        for c in range(2):
            row = TOK + 8 * (2 * k + c)
            lanes = slice(c * RB, (c + 1) * RB)
            total = y[row : row + 1] + y[row + 1 : row + 2]
            mix_out[k : k + 1, lanes] = total * SCALE / weights[k : k + 1, lanes]


def shape(dims, dtype=BF):
    return jax.ShapeDtypeStruct(dims, dtype)


def cost(flops, size):
    return pl.CostEstimate(flops=int(flops), bytes_accessed=int(size), transcendentals=0)


def whole(dims):
    return pl.BlockSpec(dims, lambda i: (0,) * len(dims))


def by_expert(n, width):
    return pl.BlockSpec((n, 1, CAP, width), lambda e: (0, e, 0, 0))


def leading(*dims):
    return pl.BlockSpec((1,) + dims, lambda e: (e,) + (0,) * len(dims))


def on_device(tokens, cotangent, zone_ids, gate_weights, gate_proj, up_proj, down_proj):
    z = lax.axis_index("hidden").astype(jnp.int32).reshape(1)
    zones, weights = zone_ids.T, gate_weights.T
    cots = (cotangent, shift(cotangent, -1), shift(cotangent, 2), shift(cotangent, 1))

    smem = pl.BlockSpec(memory_space=pltpu.SMEM)
    pay, dest = pl.pallas_call(
        route_first,
        grid=(4,),
        in_specs=[whole((2, TOK)), whole((TOK, QF))],
        out_specs=[pl.BlockSpec((8, 32, QF), lambda i: (i, 0, 0)), whole((2, TOK))],
        out_shape=[shape((OWN, 32, QF)), shape((2, TOK), jnp.int32)],
        scratch_shapes=[pltpu.VMEM((2, TOK), jnp.int32)],
        compiler_params=params(),
        cost_estimate=cost(5e8, 4e6),
        name="route_first",
    )(zones, tokens)
    got = lax.all_to_all(pay, "expert", split_axis=0, concat_axis=0, tiled=True)

    pay_rest = pl.pallas_call(
        route_rest,
        grid=(4,),
        in_specs=[smem, whole((2, TOK)), whole((2, TOK))] + [whole((TOK, QF))] * 4,
        out_specs=pl.BlockSpec((8, 32, D), lambda i: (i, 0, 0)),
        out_shape=shape((OWN, 32, D)),
        compiler_params=params(),
        cost_estimate=cost(8e8, 6e6),
        name="route_rest",
    )(z, dest, weights, *cots)
    rest = lax.all_to_all(pay_rest, "expert", split_axis=0, concat_axis=0, tiled=True)
    rest = rest.reshape(OWN, LOC, CAP, D)

    half = OWN // 2
    got = got.reshape(OWN, LOC, CAP, QF)
    top, bot = got[:half], got[half:]
    left_t = shift(top, 1)
    right_b = shift(bot, -1)
    left_b = shift(bot, 1)
    right_t = shift(top, -1)
    far_t = shift(left_t, 1)
    far_b = shift(right_b, -1)

    rows = OWN * CAP
    hid, hid_f = shape((LOC, rows, QH)), shape((LOC, rows, QH), F32)
    hid_spec = leading(rows, QH)
    x_slots, h, silu, slope = pl.pallas_call(
        gates,
        grid=(LOC,),
        in_specs=[smem, by_expert(OWN, QF)] + [by_expert(half, QF)] * 6 + [leading(D, QH)] * 2,
        out_specs=[leading(rows, D), hid_spec, hid_spec, hid_spec],
        out_shape=[shape((LOC, rows, D)), hid, hid_f, hid_f],
        scratch_shapes=[pltpu.VMEM((NZ, rows, QF), BF)],
        compiler_params=params(),
        cost_estimate=cost(2.2e9, 19e6),
        name="gates",
    )(z, got, left_t, left_b, right_t, right_b, far_t, far_b, gate_proj, up_proj)

    whole_part = shape((OWN, LOC, CAP, RA))
    half_part = shape((half, LOC, CAP, RA))
    o0, o1t, o1b, o2t, o2b, o3t, o3b, part, dg, du = pl.pallas_call(
        middle,
        grid=(LOC,),
        in_specs=[smem, by_expert(OWN, D)] + [hid_spec] * 3
        + [leading(D, QH), leading(D, QH), leading(QH, D)],
        out_specs=[by_expert(OWN, RA)] + [by_expert(half, RA)] * 6 + [by_expert(OWN, WR)]
        + [hid_spec] * 2,
        out_shape=[whole_part] + [half_part] * 6 + [shape((OWN, LOC, CAP, WR)), hid, hid],
        compiler_params=params(),
        cost_estimate=cost(3.3e9, 27e6),
        name="middle",
    )(z, rest, h, silu, slope, gate_proj, up_proj, down_proj)

    relay_t = shift(o2t, 1)
    relay_b = shift(o2b, -1)
    from_l_b = shift(o1b, 1)
    from_r_t = shift(o3t, -1)
    gate_grad, up_grad, down_grad = pl.pallas_call(
        grads,
        grid=(LOC,),
        in_specs=[leading(rows, D), by_expert(OWN, D)] + [hid_spec] * 3,
        out_specs=[leading(D, QH), leading(D, QH), leading(QH, D)],
        out_shape=[shape((LOC, D, QH)), shape((LOC, D, QH)), shape((LOC, QH, D))],
        compiler_params=params(),
        cost_estimate=cost(3.3e9, 30e6),
        name="grads",
    )(x_slots, rest, h, dg, du)
    relay_t, relay_b, down_grad = lax.optimization_barrier((relay_t, relay_b, down_grad))
    from_l_t = shift((o1t.astype(F32) + relay_t.astype(F32)).astype(BF), 1)
    from_r_b = shift((o3b.astype(F32) + relay_b.astype(F32)).astype(BF), -1)

    part_back = lax.all_to_all(
        part.reshape(OWN, 32, WR), "expert", split_axis=0, concat_axis=0, tiled=True
    ).reshape(OWN * 32, WR)

    sum_t = o0[:half].astype(F32) + from_l_t.astype(F32) + from_r_t.astype(F32)
    sum_b = o0[half:].astype(F32) + from_l_b.astype(F32) + from_r_b.astype(F32)
    sums = jnp.concatenate([sum_t.astype(BF), sum_b.astype(BF)], axis=0)
    back = lax.all_to_all(
        sums.reshape(OWN, 32, RA), "expert", split_axis=0, concat_axis=0, tiled=True
    ).reshape(OWN * 32, RA)

    y_shape = shape((TOK + 32, RB))
    y0, y1, y2, y3 = pl.pallas_call(
        pick_pairs,
        out_shape=[y_shape] * 4,
        compiler_params=params(),
        cost_estimate=cost(4e8, 3e6),
        name="pick_pairs",
    )(dest, part_back)
    ys = (y0, shift(y1, 1), shift(y2, 2), shift(y3, -1))

    input_grad, mix_t = pl.pallas_call(
        finish,
        out_shape=[shape((TOK, QF)), shape((2, TOK), F32)],
        compiler_params=params(),
        cost_estimate=cost(4e8, 3e6),
        name="finish",
    )(dest, weights, back, *ys)
    return (input_grad, mix_t.T, gate_grad, up_grad, down_grad)


def solution(mesh):
    return jax.shard_map(
        on_device,
        mesh=mesh,
        in_specs=(
            P("expert", "hidden"),
            P("expert", "hidden"),
            P("expert", None),
            P("expert", None),
            P("expert", None, "hidden"),
            P("expert", None, "hidden"),
            P("expert", "hidden", None),
        ),
        out_specs=(
            P("expert", "hidden"),
            P("expert", None),
            P("expert", None, "hidden"),
            P("expert", None, "hidden"),
            P("expert", "hidden", None),
        ),
        check_vma=False,
    )
```

```python
import jax
import jax.numpy as jnp
from jax import lax
from jax.experimental import pallas as pl
from jax.experimental.pallas import tpu as pltpu
from jax.sharding import PartitionSpec as P

D = 2048
SCALE = D ** (-0.5)
OWN = 32
NZ = 4
LOC = 4
CAP = 8
TOK = 256
QF = D // NZ
QH = 256
RA = 384
RB = QF - RA
WR = NZ * RB + 128
BF = jnp.bfloat16
F32 = jnp.float32
VMEM = 63 * 1024 * 1024


def dot(a, b, ca, cb):
    return lax.dot_general(a, b, (((ca,), (cb,)), ((), ())), preferred_element_type=F32)


def shift(x, d):
    return lax.ppermute(x, "hidden", [(i, (i + d) % NZ) for i in range(NZ)])


def params(**kw):
    return pltpu.CompilerParams(vmem_limit_bytes=VMEM, **kw)


def slots_of(dest, base, rows):
    slot = lax.broadcasted_iota(jnp.int32, (rows, TOK), 0) + base
    return slot == dest[0:1, :], slot == dest[1:2, :]


def route_first(zones, tokens, pay, dest_out, dest):
    step = pl.program_id(0)

    @pl.when(step == 0)
    def _():
        expert = lax.broadcasted_iota(jnp.int32, (OWN * LOC, TOK), 0)
        hit0 = expert == zones[0:1, :]
        hit1 = expert == zones[1:2, :]
        both = jnp.where(hit0 | hit1, 1.0, 0.0).astype(BF)
        earlier = lax.broadcasted_iota(jnp.int32, (TOK, TOK), 0) < lax.broadcasted_iota(
            jnp.int32, (TOK, TOK), 1
        )
        count = dot(both, jnp.where(earlier, 1.0, 0.0).astype(BF), 1, 0)
        rank0 = jnp.sum(jnp.where(hit0, count, 0.0), axis=0, keepdims=True)
        rank1 = jnp.sum(jnp.where(hit1, count, 0.0), axis=0, keepdims=True)
        dest[0:1, :] = zones[0:1, :] * CAP + rank0.astype(jnp.int32)
        dest[1:2, :] = zones[1:2, :] * CAP + rank1.astype(jnp.int32)
        dest_out[...] = dest[...]

    at0, at1 = slots_of(dest, step * 256, 256)
    pick = jnp.where(at0 | at1, 1.0, 0.0).astype(BF)
    pay[...] = dot(pick, tokens[...], 1, 0).astype(BF).reshape(8, 32, QF)


def route_rest(z_ref, dest, weights, c0, c1, c2, c3, pay):
    at0, at1 = slots_of(dest, pl.program_id(0) * 256, 256)
    pick = jnp.where(at0 | at1, 1.0, 0.0).astype(BF)
    w = jnp.sum(
        jnp.where(at0, weights[0:1, :], 0.0) + jnp.where(at1, weights[1:2, :], 0.0),
        axis=1,
        keepdims=True,
    )
    for off, c in enumerate((c0, c1, c2, c3)):
        dy = (dot(pick, c[...], 1, 0) * w).astype(BF)
        q = lax.rem(z_ref[0] + off, NZ)
        pay[:, :, pl.ds(pl.multiple_of(q * QF, QF), QF)] = dy.reshape(8, 32, QF)


def merged(v):
    n, r, f = v.shape
    return v.astype(F32).reshape(n * r, f).astype(BF)


def parted(v):
    return v.reshape(v.shape[0] // CAP, CAP, v.shape[1]).astype(BF)


def gates(
    z_ref, own, left_a, left_b, right_a, right_b, far_a, far_b, wg, wu,
    x_out, h_out, silu_out, slope_out, xs,
):
    pieces = ((0, (own,)), (3, (left_a, left_b)), (1, (right_a, right_b)), (2, (far_a, far_b)))
    for off, parts in pieces:
        q = lax.rem(z_ref[0] + off, NZ)
        row = 0
        for part in parts:
            n = part.shape[0] * CAP
            xs[q, row : row + n, :] = merged(part[:, 0])
            row += n
    g = u = 0.0
    for q in range(NZ):
        rows = slice(q * QF, (q + 1) * QF)
        x_out[0, :, rows] = xs[q]
        g = g + dot(xs[q], wg[0, rows, :], 1, 0)
        u = u + dot(xs[q], wu[0, rows, :], 1, 0)
    sig = jax.nn.sigmoid(g)
    silu = g * sig
    h_out[0] = (silu * u).astype(BF)
    silu_out[0] = silu
    slope_out[0] = u * sig * (1.0 + g * (1.0 - sig))


def middle(
    z_ref, rest, h_in, silu, slope, wg, wu, wd,
    o0t, o0b, o1t, o1b, o2t, o2b, o3t, o3b, part_out, dg_out, du_out,
):
    z = z_ref[0]
    h = h_in[0]
    dh = dot(merged(rest[:, 0]), wd[0], 1, 1)
    dg = (dh * slope[0]).astype(BF)
    du = (dh * silu[0]).astype(BF)
    dg_out[0] = dg
    du_out[0] = du
    mix = jnp.sum(h.astype(F32) * dh, axis=1, keepdims=True)
    high = mix.astype(BF).astype(F32)
    lane = lax.broadcasted_iota(jnp.int32, (OWN * CAP, 128), 1)
    mix = jnp.where(lane == 0, high, jnp.where(lane == 1, mix - high, 0.0))
    part_out[:, 0, :, NZ * RB :] = parted(mix)
    half = OWN * CAP // 2
    for off, top, bot in ((2, o2t, o2b), (1, o1t, o1b), (3, o3t, o3b), (0, o0t, o0b)):
        rows = pl.ds(pl.multiple_of(lax.rem(z + off, NZ) * QF, QF), QF)
        dx = dot(dg, wg[0, rows, :], 1, 1) + dot(du, wu[0, rows, :], 1, 1)
        top[:, 0] = parted(dx[:half, :RA])
        bot[:, 0] = parted(dx[half:, :RA])
        part_out[:, 0, :, off * RB : (off + 1) * RB] = parted(dx[:, RA:])


def relay_sums(a0, a1, b0, b1, a_out, b_out):
    a_out[...] = (a0[...].astype(F32) + a1[...].astype(F32)).astype(BF)
    b_out[...] = (b0[...].astype(F32) + b1[...].astype(F32)).astype(BF)


def last_sums(a0, a1, a2, b0, b1, b2, out):
    out[0] = (a0[...].astype(F32) + a1[...].astype(F32) + a2[...].astype(F32)).astype(BF)
    out[1] = (b0[...].astype(F32) + b1[...].astype(F32) + b2[...].astype(F32)).astype(BF)


def grads_down(dest, rest, h, down_out, pick_out):
    at0, at1 = slots_of(dest, pl.program_id(0) * 256, 256)
    pick_out[...] = jnp.where(at0 | at1, 1.0, 0.0).T.astype(BF)
    down_out[0] = dot(h[0], merged(rest[:, 0]), 0, 0).astype(BF)


def grads_up(x, dg, du, gate_out, up_out):
    gate_out[0] = dot(x[0], dg[0], 0, 0).astype(BF)
    up_out[0] = dot(x[0], du[0], 0, 0).astype(BF)


def pick_pairs(dest, back, y0, y1, y2, y3, ys):
    at0, at1 = slots_of(dest, 0, OWN * LOC * CAP)
    one0 = jnp.where(at0, 1.0, 0.0).astype(BF)
    one1 = jnp.where(at1, 1.0, 0.0).astype(BF)
    ys[...] = dot(one0 + one1, back[:, : NZ * RB], 0, 0)
    m0 = dot(back[:, NZ * RB :], one0, 0, 0)
    m1 = dot(back[:, NZ * RB :], one1, 0, 0)
    rows = [m[:8, c : c + RB] for m in (m0, m1) for c in range(0, TOK, RB)]
    mix = jnp.concatenate(rows, axis=0).astype(BF)
    for off, out in enumerate((y0, y1, y2, y3)):
        out[:TOK, :] = ys[:, off * RB : (off + 1) * RB].astype(BF)
        out[TOK:, :] = mix


def finish(pick, weights, back, y0, y1, y2, y3, grad_out, mix_out):
    grad_out[:, :RA] = dot(pick[...], back[...], 1, 0).astype(BF)
    y = (y0[...].astype(F32) + y2[...].astype(F32)) + (y1[...].astype(F32) + y3[...].astype(F32))
    grad_out[:, RA:] = y[:TOK].astype(BF)
    for k in range(2):
        for c in range(2):
            row = TOK + 8 * (2 * k + c)
            lanes = slice(c * RB, (c + 1) * RB)
            total = y[row : row + 1] + y[row + 1 : row + 2]
            mix_out[k : k + 1, lanes] = total * SCALE / weights[k : k + 1, lanes]


def shape(dims, dtype=BF):
    return jax.ShapeDtypeStruct(dims, dtype)


def cost(flops, size):
    return pl.CostEstimate(flops=int(flops), bytes_accessed=int(size), transcendentals=0)


def whole(dims):
    return pl.BlockSpec(dims, lambda i: (0,) * len(dims))


def by_expert(n, width):
    return pl.BlockSpec((n, 1, CAP, width), lambda e: (0, e, 0, 0))


def leading(*dims):
    return pl.BlockSpec((1,) + dims, lambda e: (e,) + (0,) * len(dims))


def on_device(tokens, cotangent, zone_ids, gate_weights, gate_proj, up_proj, down_proj):
    z = lax.axis_index("hidden").astype(jnp.int32).reshape(1)
    zones, weights = zone_ids.T, gate_weights.T
    cots = (cotangent, shift(cotangent, -1), shift(cotangent, 2), shift(cotangent, 1))

    smem = pl.BlockSpec(memory_space=pltpu.SMEM)
    pay, dest = pl.pallas_call(
        route_first,
        grid=(4,),
        in_specs=[whole((2, TOK)), whole((TOK, QF))],
        out_specs=[pl.BlockSpec((8, 32, QF), lambda i: (i, 0, 0)), whole((2, TOK))],
        out_shape=[shape((OWN, 32, QF)), shape((2, TOK), jnp.int32)],
        scratch_shapes=[pltpu.VMEM((2, TOK), jnp.int32)],
        compiler_params=params(),
        cost_estimate=cost(5e8, 4e6),
        name="route_first",
    )(zones, tokens)
    got = lax.all_to_all(pay, "expert", split_axis=0, concat_axis=0, tiled=True)

    pay_rest = pl.pallas_call(
        route_rest,
        grid=(4,),
        in_specs=[smem, whole((2, TOK)), whole((2, TOK))] + [whole((TOK, QF))] * 4,
        out_specs=pl.BlockSpec((8, 32, D), lambda i: (i, 0, 0)),
        out_shape=shape((OWN, 32, D)),
        compiler_params=params(),
        cost_estimate=cost(8e8, 6e6),
        name="route_rest",
    )(z, dest, weights, *cots)
    rest = lax.all_to_all(pay_rest, "expert", split_axis=0, concat_axis=0, tiled=True)
    rest = rest.reshape(OWN, LOC, CAP, D)

    half = OWN // 2
    got = got.reshape(OWN, LOC, CAP, QF)
    top, bot = got[:half], got[half:]
    left_t = shift(top, 1)
    right_b = shift(bot, -1)
    left_b = shift(bot, 1)
    right_t = shift(top, -1)
    far_t = shift(left_t, 1)
    far_b = shift(right_b, -1)

    rows = OWN * CAP
    hid, hid_f = shape((LOC, rows, QH)), shape((LOC, rows, QH), F32)
    hid_spec = leading(rows, QH)
    x_slots, h, silu, slope = pl.pallas_call(
        gates,
        grid=(LOC,),
        in_specs=[smem, by_expert(OWN, QF)] + [by_expert(half, QF)] * 6 + [leading(D, QH)] * 2,
        out_specs=[leading(rows, D), hid_spec, hid_spec, hid_spec],
        out_shape=[shape((LOC, rows, D)), hid, hid_f, hid_f],
        scratch_shapes=[pltpu.VMEM((NZ, rows, QF), BF)],
        compiler_params=params(),
        cost_estimate=cost(2.2e9, 19e6),
        name="gates",
    )(z, got, left_t, left_b, right_t, right_b, far_t, far_b, gate_proj, up_proj)

    half_part = shape((half, LOC, CAP, RA))
    o0t, o0b, o1t, o1b, o2t, o2b, o3t, o3b, part, dg, du = pl.pallas_call(
        middle,
        grid=(LOC,),
        in_specs=[smem, by_expert(OWN, D)] + [hid_spec] * 3
        + [leading(D, QH), leading(D, QH), leading(QH, D)],
        out_specs=[by_expert(half, RA)] * 8 + [by_expert(OWN, WR)] + [hid_spec] * 2,
        out_shape=[half_part] * 8 + [shape((OWN, LOC, CAP, WR)), hid, hid],
        compiler_params=params(),
        cost_estimate=cost(2.7e9, 27e6),
        name="middle",
    )(z, rest, h, silu, slope, gate_proj, up_proj, down_proj)

    relay_t = shift(o2t, 1)
    relay_b = shift(o2b, -1)
    from_l_b = shift(o1b, 1)
    from_r_t = shift(o3t, -1)

    part_back = lax.all_to_all(
        part.reshape(OWN, 32, WR), "expert", split_axis=0, concat_axis=0, tiled=True
    ).reshape(OWN * 32, WR)

    down_grad, pick = pl.pallas_call(
        grads_down,
        grid=(LOC,),
        in_specs=[whole((2, TOK)), by_expert(OWN, D), hid_spec],
        out_specs=[leading(QH, D), pl.BlockSpec((TOK, 256), lambda e: (0, e))],
        out_shape=[shape((LOC, QH, D)), shape((TOK, OWN * LOC * CAP))],
        compiler_params=params(),
        cost_estimate=cost(1.1e9, 10e6),
        name="grads_down",
    )(dest, rest, h)
    relay_t, relay_b, pick = lax.optimization_barrier((relay_t, relay_b, pick))

    quarter = pl.BlockSpec((half // 4, LOC, CAP, RA), lambda i: (i, 0, 0, 0))
    sum_t, sum_b = pl.pallas_call(
        relay_sums,
        grid=(4,),
        in_specs=[quarter] * 4,
        out_specs=[quarter] * 2,
        out_shape=[half_part] * 2,
        compiler_params=params(),
        cost_estimate=cost(1e6, 2.4e6),
        name="relay_sums",
    )(o1t, relay_t, o3b, relay_b)
    from_l_t = shift(sum_t, 1)
    from_r_b = shift(sum_b, -1)

    sum_t, sum_b, dg, du = lax.optimization_barrier((sum_t, sum_b, dg, du))
    gate_grad, up_grad = pl.pallas_call(
        grads_up,
        grid=(LOC,),
        in_specs=[leading(rows, D)] + [hid_spec] * 2,
        out_specs=[leading(D, QH), leading(D, QH)],
        out_shape=[shape((LOC, D, QH)), shape((LOC, D, QH))],
        compiler_params=params(),
        cost_estimate=cost(1.2e10, 20e6),
        name="grads_up",
    )(x_slots, dg, du)
    from_l_b, from_r_t, up_grad = lax.optimization_barrier((from_l_b, from_r_t, up_grad))
    sums = pl.pallas_call(
        last_sums,
        grid=(4,),
        in_specs=[quarter] * 6,
        out_specs=pl.BlockSpec((2, half // 4, LOC, CAP, RA), lambda i: (0, i, 0, 0, 0)),
        out_shape=shape((2, half, LOC, CAP, RA)),
        compiler_params=params(),
        cost_estimate=cost(2e6, 3.2e6),
        name="last_sums",
    )(o0t, from_l_t, from_r_t, o0b, from_l_b, from_r_b)
    back = lax.all_to_all(
        sums.reshape(OWN, 32, RA), "expert", split_axis=0, concat_axis=0, tiled=True
    ).reshape(OWN * 32, RA)

    y_shape = shape((TOK + 32, RB))
    y0, y1, y2, y3 = pl.pallas_call(
        pick_pairs,
        in_specs=[pl.BlockSpec(memory_space=pltpu.VMEM)] * 2,
        out_shape=[y_shape] * 4,
        scratch_shapes=[pltpu.VMEM((TOK, NZ * RB), F32)],
        compiler_params=params(),
        cost_estimate=cost(4e8, 3e6),
        name="pick_pairs",
    )(dest, part_back)
    ys = (y0, shift(y1, 1), shift(y2, 2), shift(y3, -1))

    input_grad, mix_t = pl.pallas_call(
        finish,
        out_shape=[shape((TOK, QF)), shape((2, TOK), F32)],
        compiler_params=params(),
        cost_estimate=cost(4e8, 3e6),
        name="finish",
    )(pick, weights, back, *ys)
    return (input_grad, mix_t.T, gate_grad, up_grad, down_grad)


def solution(mesh):
    return jax.shard_map(
        on_device,
        mesh=mesh,
        in_specs=(
            P("expert", "hidden"),
            P("expert", "hidden"),
            P("expert", None),
            P("expert", None),
            P("expert", None, "hidden"),
            P("expert", None, "hidden"),
            P("expert", "hidden", None),
        ),
        out_specs=(
            P("expert", "hidden"),
            P("expert", None),
            P("expert", None, "hidden"),
            P("expert", None, "hidden"),
            P("expert", "hidden", None),
        ),
        check_vma=False,
    )
```

```python
import jax
import jax.numpy as jnp
from jax import lax
from jax.experimental import pallas as pl
from jax.experimental.pallas import tpu as pltpu
from jax.sharding import PartitionSpec as P

D = 2048
SCALE = D ** (-0.5)
OWN = 32
NZ = 4
LOC = 4
CAP = 8
TOK = 256
QF = D // NZ
QH = 256
RA = 384
RB = QF - RA
WR = NZ * RB + 128
BF = jnp.bfloat16
F32 = jnp.float32
MIB = 1024 * 1024
ROUTE = 56
LAST = 56


def dot(a, b, ca, cb):
    return lax.dot_general(a, b, (((ca,), (cb,)), ((), ())), preferred_element_type=F32)


def shift(x, d):
    return lax.ppermute(x, "hidden", [(i, (i + d) % NZ) for i in range(NZ)])


def params(mib=63):
    return pltpu.CompilerParams(vmem_limit_bytes=mib * MIB)


def slots_of(dest, base, rows):
    slot = lax.broadcasted_iota(jnp.int32, (rows, TOK), 0) + base
    return slot == dest[0:1, :], slot == dest[1:2, :]


def route_first(zones, tokens, pay, dest_out, dest):
    step = pl.program_id(0)

    @pl.when(step == 0)
    def _():
        expert = lax.broadcasted_iota(jnp.int32, (OWN * LOC, TOK), 0)
        hit0 = expert == zones[0:1, :]
        hit1 = expert == zones[1:2, :]
        both = jnp.where(hit0 | hit1, 1.0, 0.0).astype(BF)
        earlier = lax.broadcasted_iota(jnp.int32, (TOK, TOK), 0) < lax.broadcasted_iota(
            jnp.int32, (TOK, TOK), 1
        )
        count = dot(both, jnp.where(earlier, 1.0, 0.0).astype(BF), 1, 0)
        rank0 = jnp.sum(jnp.where(hit0, count, 0.0), axis=0, keepdims=True)
        rank1 = jnp.sum(jnp.where(hit1, count, 0.0), axis=0, keepdims=True)
        dest[0:1, :] = zones[0:1, :] * CAP + rank0.astype(jnp.int32)
        dest[1:2, :] = zones[1:2, :] * CAP + rank1.astype(jnp.int32)
        dest_out[...] = dest[...]

    at0, at1 = slots_of(dest, step * 256, 256)
    pick = jnp.where(at0 | at1, 1.0, 0.0).astype(BF)
    pay[...] = dot(pick, tokens[...], 1, 0).astype(BF).reshape(8, 32, QF)


def picked(dest, weights):
    at0, at1 = slots_of(dest, pl.program_id(0) * 256, 256)
    pick = jnp.where(at0 | at1, 1.0, 0.0).astype(BF)
    w = jnp.sum(
        jnp.where(at0, weights[0:1, :], 0.0) + jnp.where(at1, weights[1:2, :], 0.0),
        axis=1,
        keepdims=True,
    )
    return pick, w


def route_near(z_ref, dest, weights, c0, c1, c3, pay):
    pick, w = picked(dest, weights)
    for off, c in ((0, c0), (1, c1), (3, c3)):
        dy = (dot(pick, c[...], 1, 0) * w).astype(BF)
        q = lax.rem(z_ref[0] + off, NZ)
        pay[:, :, pl.ds(pl.multiple_of(q * QF, QF), QF)] = dy.reshape(8, 32, QF)


def route_far(z_ref, dest, weights, c2, near, pay):
    pick, w = picked(dest, weights)
    pay[...] = (dot(pick, c2[...], 1, 0) * w).astype(BF).reshape(8, 32, QF)


def merged(v):
    n, r, f = v.shape
    return v.astype(F32).reshape(n * r, f).astype(BF)


def parted(v):
    return v.reshape(v.shape[0] // CAP, CAP, v.shape[1]).astype(BF)


def gates(
    z_ref, own, left_a, left_b, right_a, right_b, far_a, far_b, wg, wu,
    x_out, h_out, silu_out, slope_out, xs,
):
    pieces = ((0, (own,)), (3, (left_a, left_b)), (1, (right_a, right_b)), (2, (far_a, far_b)))
    for off, parts in pieces:
        q = lax.rem(z_ref[0] + off, NZ)
        row = 0
        for part in parts:
            n = part.shape[0] * CAP
            xs[q, row : row + n, :] = merged(part[:, 0])
            row += n
    g = u = 0.0
    for q in range(NZ):
        rows = slice(q * QF, (q + 1) * QF)
        x_out[0, :, rows] = xs[q]
        g = g + dot(xs[q], wg[0, rows, :], 1, 0)
        u = u + dot(xs[q], wu[0, rows, :], 1, 0)
    sig = jax.nn.sigmoid(g)
    silu = g * sig
    h_out[0] = (silu * u).astype(BF)
    silu_out[0] = silu
    slope_out[0] = u * sig * (1.0 + g * (1.0 - sig))


def middle(
    z_ref, rest, h_in, silu, slope, wg, wu, wd,
    o0t, o0b, o1t, o1b, o2t, o2b, o3t, o3b, part_out, dg_out, du_out,
):
    z = z_ref[0]
    h = h_in[0]
    dh = dot(merged(rest[:, 0]), wd[0], 1, 1)
    dg = (dh * slope[0]).astype(BF)
    du = (dh * silu[0]).astype(BF)
    dg_out[0] = dg
    du_out[0] = du
    mix = jnp.sum(h.astype(F32) * dh, axis=1, keepdims=True)
    high = mix.astype(BF).astype(F32)
    lane = lax.broadcasted_iota(jnp.int32, (OWN * CAP, 128), 1)
    mix = jnp.where(lane == 0, high, jnp.where(lane == 1, mix - high, 0.0))
    part_out[:, 0, :, NZ * RB :] = parted(mix)
    half = OWN * CAP // 2
    for off, top, bot in ((2, o2t, o2b), (1, o1t, o1b), (3, o3t, o3b), (0, o0t, o0b)):
        rows = pl.ds(pl.multiple_of(lax.rem(z + off, NZ) * QF, QF), QF)
        dx = dot(dg, wg[0, rows, :], 1, 1) + dot(du, wu[0, rows, :], 1, 1)
        top[:, 0] = parted(dx[:half, :RA])
        bot[:, 0] = parted(dx[half:, :RA])
        part_out[:, 0, :, off * RB : (off + 1) * RB] = parted(dx[:, RA:])


def grads_down(dest, rest, h, down_out, pick_out):
    at0, at1 = slots_of(dest, pl.program_id(0) * 256, 256)
    pick_out[...] = jnp.where(at0 | at1, 1.0, 0.0).T.astype(BF)
    down_out[0] = dot(h[0], merged(rest[:, 0]), 0, 0).astype(BF)


def grads_up(x, dg, du, gate_out, up_out):
    gate_out[0] = dot(x[0], dg[0], 0, 0).astype(BF)
    up_out[0] = dot(x[0], du[0], 0, 0).astype(BF)


def pick_pairs(dest, back, y0, y1, y2, y3, ys):
    at0, at1 = slots_of(dest, 0, OWN * LOC * CAP)
    one0 = jnp.where(at0, 1.0, 0.0).astype(BF)
    one1 = jnp.where(at1, 1.0, 0.0).astype(BF)
    ys[...] = dot(one0 + one1, back[:, : NZ * RB], 0, 0)
    m0 = dot(back[:, NZ * RB :], one0, 0, 0)
    m1 = dot(back[:, NZ * RB :], one1, 0, 0)
    rows = [m[:8, c : c + RB] for m in (m0, m1) for c in range(0, TOK, RB)]
    mix = jnp.concatenate(rows, axis=0).astype(BF)
    for off, out in enumerate((y0, y1, y2, y3)):
        out[:TOK, :] = ys[:, off * RB : (off + 1) * RB].astype(BF)
        out[TOK:, :] = mix


def finish(pick, weights, back, y0, y1, y2, y3, grad_out, mix_out):
    grad_out[:, :RA] = dot(pick[...], back[...], 1, 0).astype(BF)
    y = (y0[...].astype(F32) + y2[...].astype(F32)) + (y1[...].astype(F32) + y3[...].astype(F32))
    grad_out[:, RA:] = y[:TOK].astype(BF)
    for k in range(2):
        for c in range(2):
            row = TOK + 8 * (2 * k + c)
            lanes = slice(c * RB, (c + 1) * RB)
            total = y[row : row + 1] + y[row + 1 : row + 2]
            mix_out[k : k + 1, lanes] = total * SCALE / weights[k : k + 1, lanes]


def shape(dims, dtype=BF):
    return pltpu.HBM(dims, dtype)


def cost(flops, size):
    return pl.CostEstimate(flops=int(flops), bytes_accessed=int(size), transcendentals=0)


def whole(dims):
    return pl.BlockSpec(dims, lambda i: (0,) * len(dims))


def by_expert(n, width):
    return pl.BlockSpec((n, 1, CAP, width), lambda e: (0, e, 0, 0))


def leading(*dims):
    return pl.BlockSpec((1,) + dims, lambda e: (e,) + (0,) * len(dims))


def on_device(tokens, cotangent, zone_ids, gate_weights, gate_proj, up_proj, down_proj):
    z = lax.axis_index("hidden").astype(jnp.int32).reshape(1)
    zones, weights = zone_ids.T, gate_weights.T
    smem = pl.BlockSpec(memory_space=pltpu.SMEM)
    pay, dest = pl.pallas_call(
        route_first,
        grid=(4,),
        in_specs=[whole((2, TOK)), whole((TOK, QF))],
        out_specs=[pl.BlockSpec((8, 32, QF), lambda i: (i, 0, 0)), whole((2, TOK))],
        out_shape=[shape((OWN, 32, QF)), shape((2, TOK), jnp.int32)],
        scratch_shapes=[pltpu.VMEM((2, TOK), jnp.int32)],
        compiler_params=params(),
        cost_estimate=cost(5e8, 4e6),
        name="route_first",
    )(zones, tokens)
    got = lax.all_to_all(pay, "expert", split_axis=0, concat_axis=0, tiled=True)

    c1, c2, c3 = shift(cotangent, -1), shift(cotangent, 2), shift(cotangent, 1)
    c1, c2, c3 = (pltpu.with_memory_space_constraint(c, pltpu.VMEM) for c in (c1, c2, c3))
    pay_rest = pl.pallas_call(
        route_near,
        grid=(4,),
        in_specs=[smem, whole((2, TOK)), whole((2, TOK))] + [whole((TOK, QF))] * 3,
        out_specs=pl.BlockSpec((8, 32, D), lambda i: (i, 0, 0)),
        out_shape=shape((OWN, 32, D)),
        compiler_params=params(ROUTE),
        cost_estimate=cost(6e8, 5e6),
        name="route_near",
    )(z, dest, weights, cotangent, c1, c3)
    fixed = pl.BlockSpec((2, TOK), lambda i, z: (0, 0))
    pay_rest = pl.pallas_call(
        route_far,
        grid_spec=pltpu.PrefetchScalarGridSpec(
            num_scalar_prefetch=1,
            grid=(4,),
            in_specs=[
                fixed,
                fixed,
                pl.BlockSpec((TOK, QF), lambda i, z: (0, 0)),
                pl.BlockSpec(memory_space=pl.ANY),
            ],
            out_specs=pl.BlockSpec((8, 32, QF), lambda i, z: (i, 0, lax.rem(z[0] + 2, NZ))),
        ),
        out_shape=shape((OWN, 32, D)),
        input_output_aliases={4: 0},
        compiler_params=params(ROUTE),
        cost_estimate=cost(2e8, 2e6),
        name="route_far",
    )(z, dest, weights, c2, pay_rest)
    rest = lax.all_to_all(pay_rest, "expert", split_axis=0, concat_axis=0, tiled=True)
    rest = rest.reshape(OWN, LOC, CAP, D)

    half = OWN // 2
    got = got.reshape(OWN, LOC, CAP, QF)
    top, bot = got[:half], got[half:]
    left_t = shift(top, 1)
    right_b = shift(bot, -1)
    left_b = shift(bot, 1)
    right_t = shift(top, -1)
    far_t = shift(left_t, 1)
    far_b = shift(right_b, -1)

    left_b, right_t, far_t, far_b = (
        pltpu.with_memory_space_constraint(v, pltpu.VMEM) for v in (left_b, right_t, far_t, far_b)
    )
    rows = OWN * CAP
    hid, hid_f = shape((LOC, rows, QH)), shape((LOC, rows, QH), F32)
    hid_spec = leading(rows, QH)
    x_slots, h, silu, slope = pl.pallas_call(
        gates,
        grid=(LOC,),
        in_specs=[smem, by_expert(OWN, QF)] + [by_expert(half, QF)] * 6 + [leading(D, QH)] * 2,
        out_specs=[leading(rows, D), hid_spec, hid_spec, hid_spec],
        out_shape=[shape((LOC, rows, D)), hid, hid_f, hid_f],
        scratch_shapes=[pltpu.VMEM((NZ, rows, QF), BF)],
        compiler_params=params(56),
        cost_estimate=cost(2.2e9, 19e6),
        name="gates",
    )(z, got, left_t, left_b, right_t, right_b, far_t, far_b, gate_proj, up_proj)

    half_part = shape((half, LOC, CAP, RA))
    o0t, o0b, o1t, o1b, o2t, o2b, o3t, o3b, part, dg, du = pl.pallas_call(
        middle,
        grid=(LOC,),
        in_specs=[smem, by_expert(OWN, D)] + [hid_spec] * 3
        + [leading(D, QH), leading(D, QH), leading(QH, D)],
        out_specs=[by_expert(half, RA)] * 8 + [by_expert(OWN, WR)] + [hid_spec] * 2,
        out_shape=[half_part] * 8 + [shape((OWN, LOC, CAP, WR)), hid, hid],
        compiler_params=params(),
        cost_estimate=cost(2.7e9, 27e6),
        name="middle",
    )(z, rest, h, silu, slope, gate_proj, up_proj, down_proj)

    relay_t = shift(o2t, 1)
    relay_b = shift(o2b, -1)
    from_l_b = shift(o1b, 1)
    from_r_t = shift(o3t, -1)

    part_back = lax.all_to_all(
        part.reshape(OWN, 32, WR), "expert", split_axis=0, concat_axis=0, tiled=True
    ).reshape(OWN * 32, WR)

    down_grad, pick = pl.pallas_call(
        grads_down,
        grid=(LOC,),
        in_specs=[whole((2, TOK)), by_expert(OWN, D), hid_spec],
        out_specs=[leading(QH, D), pl.BlockSpec((TOK, 256), lambda e: (0, e))],
        out_shape=[shape((LOC, QH, D)), shape((TOK, OWN * LOC * CAP))],
        compiler_params=params(),
        cost_estimate=cost(1.1e9, 10e6),
        name="grads_down",
    )(dest, rest, h)
    relay_t, relay_b, pick = lax.optimization_barrier((relay_t, relay_b, pick))

    sum_t = (o1t.astype(F32) + relay_t.astype(F32)).astype(BF)
    sum_b = (o3b.astype(F32) + relay_b.astype(F32)).astype(BF)
    from_l_t = shift(sum_t, 1)
    from_r_b = shift(sum_b, -1)

    sum_t, sum_b, dg, du = lax.optimization_barrier((sum_t, sum_b, dg, du))
    gate_grad, up_grad = pl.pallas_call(
        grads_up,
        grid=(LOC,),
        in_specs=[leading(rows, D)] + [hid_spec] * 2,
        out_specs=[leading(D, QH), leading(D, QH)],
        out_shape=[shape((LOC, D, QH)), shape((LOC, D, QH))],
        compiler_params=params(),
        cost_estimate=cost(1.2e10, 20e6),
        name="grads_up",
    )(x_slots, dg, du)
    from_l_b, from_r_t, up_grad = lax.optimization_barrier((from_l_b, from_r_t, up_grad))
    sum_t = o0t.astype(F32) + from_l_t.astype(F32) + from_r_t.astype(F32)
    sum_b = o0b.astype(F32) + from_l_b.astype(F32) + from_r_b.astype(F32)
    sums = jnp.concatenate([sum_t.astype(BF), sum_b.astype(BF)], axis=0)
    back = lax.all_to_all(
        sums.reshape(OWN, 32, RA), "expert", split_axis=0, concat_axis=0, tiled=True
    ).reshape(OWN * 32, RA)

    y_shape = shape((TOK + 32, RB))
    y0, y1, y2, y3 = pl.pallas_call(
        pick_pairs,
        in_specs=[pl.BlockSpec(memory_space=pltpu.VMEM)] * 2,
        out_shape=[y_shape] * 4,
        scratch_shapes=[pltpu.VMEM((TOK, NZ * RB), F32)],
        compiler_params=params(),
        cost_estimate=cost(4e8, 3e6),
        name="pick_pairs",
    )(dest, part_back)
    ys = (y0, shift(y1, 1), shift(y2, 2), shift(y3, -1))

    back = pltpu.with_memory_space_constraint(back, pltpu.VMEM)
    input_grad, mix_t = pl.pallas_call(
        finish,
        out_specs=[pl.BlockSpec(memory_space=pltpu.VMEM)] * 2,
        out_shape=[jax.ShapeDtypeStruct((TOK, QF), BF), jax.ShapeDtypeStruct((2, TOK), F32)],
        compiler_params=params(LAST),
        cost_estimate=cost(4e8, 3e6),
        name="finish",
    )(pick, weights, back, *ys)
    return (input_grad, mix_t.T, gate_grad, up_grad, down_grad)


def solution(mesh):
    return jax.shard_map(
        on_device,
        mesh=mesh,
        in_specs=(
            P("expert", "hidden"),
            P("expert", "hidden"),
            P("expert", None),
            P("expert", None),
            P("expert", None, "hidden"),
            P("expert", None, "hidden"),
            P("expert", "hidden", None),
        ),
        out_specs=(
            P("expert", "hidden"),
            P("expert", None),
            P("expert", None, "hidden"),
            P("expert", None, "hidden"),
            P("expert", "hidden", None),
        ),
        check_vma=False,
    )
```

```python
import jax
import jax.numpy as jnp
from jax import lax
from jax.experimental import pallas as pl
from jax.experimental.pallas import tpu as pltpu
from jax.sharding import PartitionSpec as P

D = 2048
SCALE = D ** (-0.5)
OWN = 32
NZ = 4
LOC = 4
CAP = 8
TOK = 256
QF = D // NZ
QH = 256
RA = 384
RB = QF - RA
WR = NZ * RB + 128
BF = jnp.bfloat16
F32 = jnp.float32
MIB = 1024 * 1024
ROUTE = 56
LAST = 56


def dot(a, b, ca, cb):
    return lax.dot_general(a, b, (((ca,), (cb,)), ((), ())), preferred_element_type=F32)


def shift(x, d):
    return lax.ppermute(x, "hidden", [(i, (i + d) % NZ) for i in range(NZ)])


def params(mib=63):
    return pltpu.CompilerParams(vmem_limit_bytes=mib * MIB)


def slots_of(dest, base, rows):
    slot = lax.broadcasted_iota(jnp.int32, (rows, TOK), 0) + base
    return slot == dest[0:1, :], slot == dest[1:2, :]


def route_first(zones, tokens, pay, dest_out, dest):
    step = pl.program_id(0)

    @pl.when(step == 0)
    def _():
        expert = lax.broadcasted_iota(jnp.int32, (OWN * LOC, TOK), 0)
        hit0 = expert == zones[0:1, :]
        hit1 = expert == zones[1:2, :]
        both = jnp.where(hit0 | hit1, 1.0, 0.0).astype(BF)
        earlier = lax.broadcasted_iota(jnp.int32, (TOK, TOK), 0) < lax.broadcasted_iota(
            jnp.int32, (TOK, TOK), 1
        )
        count = dot(both, jnp.where(earlier, 1.0, 0.0).astype(BF), 1, 0)
        rank0 = jnp.sum(jnp.where(hit0, count, 0.0), axis=0, keepdims=True)
        rank1 = jnp.sum(jnp.where(hit1, count, 0.0), axis=0, keepdims=True)
        dest[0:1, :] = zones[0:1, :] * CAP + rank0.astype(jnp.int32)
        dest[1:2, :] = zones[1:2, :] * CAP + rank1.astype(jnp.int32)
        dest_out[...] = dest[...]

    at0, at1 = slots_of(dest, step * 256, 256)
    pick = jnp.where(at0 | at1, 1.0, 0.0).astype(BF)
    pay[...] = dot(pick, tokens[...], 1, 0).astype(BF).reshape(8, 32, QF)


def picked(dest, weights):
    at0, at1 = slots_of(dest, pl.program_id(0) * 256, 256)
    pick = jnp.where(at0 | at1, 1.0, 0.0).astype(BF)
    w = jnp.sum(
        jnp.where(at0, weights[0:1, :], 0.0) + jnp.where(at1, weights[1:2, :], 0.0),
        axis=1,
        keepdims=True,
    )
    return pick, w


def route_rest(z_ref, dest, weights, c0, c1, c2, c3, pay):
    pick, w = picked(dest, weights)
    for off, c in enumerate((c0, c1, c2, c3)):
        dy = (dot(pick, c[...], 1, 0) * w).astype(BF)
        q = lax.rem(z_ref[0] + off, NZ)
        pay[:, :, pl.ds(pl.multiple_of(q * QF, QF), QF)] = dy.reshape(8, 32, QF)


def merged(v):
    n, r, f = v.shape
    return v.astype(F32).reshape(n * r, f).astype(BF)


def parted(v):
    return v.reshape(v.shape[0] // CAP, CAP, v.shape[1]).astype(BF)


def gates(
    z_ref, own, left_a, left_b, right_a, right_b, far_a, far_b, wg, wu,
    x_out, h_out, silu_out, slope_out, xs,
):
    pieces = ((0, (own,)), (3, (left_a, left_b)), (1, (right_a, right_b)), (2, (far_a, far_b)))
    for off, parts in pieces:
        q = lax.rem(z_ref[0] + off, NZ)
        row = 0
        for part in parts:
            n = part.shape[0] * CAP
            xs[q, row : row + n, :] = merged(part[:, 0])
            row += n
    g = u = 0.0
    for q in range(NZ):
        rows = slice(q * QF, (q + 1) * QF)
        x_out[0, :, rows] = xs[q]
        g = g + dot(xs[q], wg[0, rows, :], 1, 0)
        u = u + dot(xs[q], wu[0, rows, :], 1, 0)
    sig = jax.nn.sigmoid(g)
    silu = g * sig
    h_out[0] = (silu * u).astype(BF)
    silu_out[0] = silu
    slope_out[0] = u * sig * (1.0 + g * (1.0 - sig))


def middle(
    z_ref, rest, h_in, silu, slope, wg, wu, wd,
    o0t, o0b, o1t, o1b, o2t, o2b, o3t, o3b, part_out, dg_out, du_out,
):
    z = z_ref[0]
    h = h_in[0]
    dh = dot(merged(rest[:, 0]), wd[0], 1, 1)
    dg = (dh * slope[0]).astype(BF)
    du = (dh * silu[0]).astype(BF)
    dg_out[0] = dg
    du_out[0] = du
    mix = jnp.sum(h.astype(F32) * dh, axis=1, keepdims=True)
    high = mix.astype(BF).astype(F32)
    lane = lax.broadcasted_iota(jnp.int32, (OWN * CAP, 128), 1)
    mix = jnp.where(lane == 0, high, jnp.where(lane == 1, mix - high, 0.0))
    part_out[:, 0, :, NZ * RB :] = parted(mix)
    half = OWN * CAP // 2
    for off, top, bot in ((2, o2t, o2b), (1, o1t, o1b), (3, o3t, o3b), (0, o0t, o0b)):
        rows = pl.ds(pl.multiple_of(lax.rem(z + off, NZ) * QF, QF), QF)
        dx = dot(dg, wg[0, rows, :], 1, 1) + dot(du, wu[0, rows, :], 1, 1)
        top[:, 0] = parted(dx[:half, :RA])
        bot[:, 0] = parted(dx[half:, :RA])
        part_out[:, 0, :, off * RB : (off + 1) * RB] = parted(dx[:, RA:])


def grads_down(dest, rest, h, down_out, pick_out):
    at0, at1 = slots_of(dest, pl.program_id(0) * 256, 256)
    pick_out[...] = jnp.where(at0 | at1, 1.0, 0.0).T.astype(BF)
    down_out[0] = dot(h[0], merged(rest[:, 0]), 0, 0).astype(BF)


def grads_up(x, dg, du, gate_out, up_out):
    gate_out[0] = dot(x[0], dg[0], 0, 0).astype(BF)
    up_out[0] = dot(x[0], du[0], 0, 0).astype(BF)


def pick_pairs(dest, back, y0, y1, y2, y3, ys):
    at0, at1 = slots_of(dest, 0, OWN * LOC * CAP)
    one0 = jnp.where(at0, 1.0, 0.0).astype(BF)
    one1 = jnp.where(at1, 1.0, 0.0).astype(BF)
    ys[...] = dot(one0 + one1, back[:, : NZ * RB], 0, 0)
    m0 = dot(back[:, NZ * RB :], one0, 0, 0)
    m1 = dot(back[:, NZ * RB :], one1, 0, 0)
    rows = [m[:8, c : c + RB] for m in (m0, m1) for c in range(0, TOK, RB)]
    mix = jnp.concatenate(rows, axis=0).astype(BF)
    for off, out in enumerate((y0, y1, y2, y3)):
        out[:TOK, :] = ys[:, off * RB : (off + 1) * RB].astype(BF)
        out[TOK:, :] = mix


def finish(pick, weights, back, y0, y1, y2, y3, grad_out, mix_out):
    grad_out[:, :RA] = dot(pick[...], back[...], 1, 0).astype(BF)
    y = (y0[...].astype(F32) + y2[...].astype(F32)) + (y1[...].astype(F32) + y3[...].astype(F32))
    grad_out[:, RA:] = y[:TOK].astype(BF)
    for k in range(2):
        for c in range(2):
            row = TOK + 8 * (2 * k + c)
            lanes = slice(c * RB, (c + 1) * RB)
            total = y[row : row + 1] + y[row + 1 : row + 2]
            mix_out[k : k + 1, lanes] = total * SCALE / weights[k : k + 1, lanes]


def shape(dims, dtype=BF):
    return pltpu.HBM(dims, dtype)


def cost(flops, size):
    return pl.CostEstimate(flops=int(flops), bytes_accessed=int(size), transcendentals=0)


def whole(dims):
    return pl.BlockSpec(dims, lambda i: (0,) * len(dims))


def by_expert(n, width):
    return pl.BlockSpec((n, 1, CAP, width), lambda e: (0, e, 0, 0))


def leading(*dims):
    return pl.BlockSpec((1,) + dims, lambda e: (e,) + (0,) * len(dims))


def on_device(tokens, cotangent, zone_ids, gate_weights, gate_proj, up_proj, down_proj):
    z = lax.axis_index("hidden").astype(jnp.int32).reshape(1)
    zones, weights = zone_ids.T, gate_weights.T
    smem = pl.BlockSpec(memory_space=pltpu.SMEM)
    pay, dest = pl.pallas_call(
        route_first,
        grid=(4,),
        in_specs=[whole((2, TOK)), whole((TOK, QF))],
        out_specs=[pl.BlockSpec((8, 32, QF), lambda i: (i, 0, 0)), whole((2, TOK))],
        out_shape=[shape((OWN, 32, QF)), shape((2, TOK), jnp.int32)],
        scratch_shapes=[pltpu.VMEM((2, TOK), jnp.int32)],
        compiler_params=params(),
        cost_estimate=cost(5e8, 4e6),
        name="route_first",
    )(zones, tokens)
    got = lax.all_to_all(pay, "expert", split_axis=0, concat_axis=0, tiled=True)

    c1, c2, c3 = shift(cotangent, -1), shift(cotangent, 2), shift(cotangent, 1)
    c1, c2, c3 = (pltpu.with_memory_space_constraint(c, pltpu.VMEM) for c in (c1, c2, c3))
    pay_rest = pl.pallas_call(
        route_rest,
        grid=(4,),
        in_specs=[smem, whole((2, TOK)), whole((2, TOK))] + [whole((TOK, QF))] * 4,
        out_specs=pl.BlockSpec((8, 32, D), lambda i: (i, 0, 0)),
        out_shape=shape((OWN, 32, D)),
        compiler_params=params(ROUTE),
        cost_estimate=cost(8e8, 6e6),
        name="route_rest",
    )(z, dest, weights, cotangent, c1, c2, c3)
    rest = lax.all_to_all(pay_rest, "expert", split_axis=0, concat_axis=0, tiled=True)
    rest = rest.reshape(OWN, LOC, CAP, D)

    half = OWN // 2
    got = got.reshape(OWN, LOC, CAP, QF)
    top, bot = got[:half], got[half:]
    left_t = shift(top, 1)
    right_b = shift(bot, -1)
    left_b = shift(bot, 1)
    right_t = shift(top, -1)
    far_t = shift(left_t, 1)
    far_b = shift(right_b, -1)

    left_b, right_t, far_t, far_b = (
        pltpu.with_memory_space_constraint(v, pltpu.VMEM) for v in (left_b, right_t, far_t, far_b)
    )
    rows = OWN * CAP
    hid, hid_f = shape((LOC, rows, QH)), shape((LOC, rows, QH), F32)
    hid_spec = leading(rows, QH)
    x_slots, h, silu, slope = pl.pallas_call(
        gates,
        grid=(LOC,),
        in_specs=[smem, by_expert(OWN, QF)] + [by_expert(half, QF)] * 6 + [leading(D, QH)] * 2,
        out_specs=[leading(rows, D), hid_spec, hid_spec, hid_spec],
        out_shape=[shape((LOC, rows, D)), hid, hid_f, hid_f],
        scratch_shapes=[pltpu.VMEM((NZ, rows, QF), BF)],
        compiler_params=params(56),
        cost_estimate=cost(2.2e9, 19e6),
        name="gates",
    )(z, got, left_t, left_b, right_t, right_b, far_t, far_b, gate_proj, up_proj)

    half_part = shape((half, LOC, CAP, RA))
    o0t, o0b, o1t, o1b, o2t, o2b, o3t, o3b, part, dg, du = pl.pallas_call(
        middle,
        grid=(LOC,),
        in_specs=[smem, by_expert(OWN, D)] + [hid_spec] * 3
        + [leading(D, QH), leading(D, QH), leading(QH, D)],
        out_specs=[by_expert(half, RA)] * 8 + [by_expert(OWN, WR)] + [hid_spec] * 2,
        out_shape=[half_part] * 8 + [shape((OWN, LOC, CAP, WR)), hid, hid],
        compiler_params=params(),
        cost_estimate=cost(2.7e9, 27e6),
        name="middle",
    )(z, rest, h, silu, slope, gate_proj, up_proj, down_proj)

    relay_t = shift(o2t, 1)
    relay_b = shift(o2b, -1)
    from_l_b = shift(o1b, 1)
    from_r_t = shift(o3t, -1)

    part_back = lax.all_to_all(
        part.reshape(OWN, 32, WR), "expert", split_axis=0, concat_axis=0, tiled=True
    ).reshape(OWN * 32, WR)


    sum_t = (o1t.astype(F32) + relay_t.astype(F32)).astype(BF)
    sum_b = (o3b.astype(F32) + relay_b.astype(F32)).astype(BF)
    from_l_t = shift(sum_t, 1)
    from_r_b = shift(sum_b, -1)

    sum_t, sum_b, dg, du = lax.optimization_barrier((sum_t, sum_b, dg, du))
    gate_grad, up_grad = pl.pallas_call(
        grads_up,
        grid=(LOC,),
        in_specs=[leading(rows, D)] + [hid_spec] * 2,
        out_specs=[leading(D, QH), leading(D, QH)],
        out_shape=[shape((LOC, D, QH)), shape((LOC, D, QH))],
        compiler_params=params(),
        cost_estimate=cost(1.2e10, 20e6),
        name="grads_up",
    )(x_slots, dg, du)
    from_l_b, from_r_t, up_grad = lax.optimization_barrier((from_l_b, from_r_t, up_grad))
    sum_t = o0t.astype(F32) + from_l_t.astype(F32) + from_r_t.astype(F32)
    sum_b = o0b.astype(F32) + from_l_b.astype(F32) + from_r_b.astype(F32)
    sums = jnp.concatenate([sum_t.astype(BF), sum_b.astype(BF)], axis=0)
    sums, h = lax.optimization_barrier((sums, h))
    down_grad, pick = pl.pallas_call(
        grads_down,
        grid=(LOC,),
        in_specs=[whole((2, TOK)), by_expert(OWN, D), hid_spec],
        out_specs=[leading(QH, D), pl.BlockSpec((TOK, 256), lambda e: (0, e))],
        out_shape=[shape((LOC, QH, D)), shape((TOK, OWN * LOC * CAP))],
        compiler_params=params(),
        cost_estimate=cost(1.1e9, 10e6),
        name="grads_down",
    )(dest, rest, h)
    back = lax.all_to_all(
        sums.reshape(OWN, 32, RA), "expert", split_axis=0, concat_axis=0, tiled=True
    ).reshape(OWN * 32, RA)

    y_shape = shape((TOK + 32, RB))
    y0, y1, y2, y3 = pl.pallas_call(
        pick_pairs,
        in_specs=[pl.BlockSpec(memory_space=pltpu.VMEM)] * 2,
        out_shape=[y_shape] * 4,
        scratch_shapes=[pltpu.VMEM((TOK, NZ * RB), F32)],
        compiler_params=params(),
        cost_estimate=cost(4e8, 3e6),
        name="pick_pairs",
    )(dest, part_back)
    ys = (y0, shift(y1, 1), shift(y2, 2), shift(y3, -1))

    back = pltpu.with_memory_space_constraint(back, pltpu.VMEM)
    input_grad, mix_t = pl.pallas_call(
        finish,
        out_specs=[pl.BlockSpec(memory_space=pltpu.VMEM)] * 2,
        out_shape=[jax.ShapeDtypeStruct((TOK, QF), BF), jax.ShapeDtypeStruct((2, TOK), F32)],
        compiler_params=params(LAST),
        cost_estimate=cost(4e8, 3e6),
        name="finish",
    )(pick, weights, back, *ys)
    return (input_grad, mix_t.T, gate_grad, up_grad, down_grad)


def solution(mesh):
    return jax.shard_map(
        on_device,
        mesh=mesh,
        in_specs=(
            P("expert", "hidden"),
            P("expert", "hidden"),
            P("expert", None),
            P("expert", None),
            P("expert", None, "hidden"),
            P("expert", None, "hidden"),
            P("expert", "hidden", None),
        ),
        out_specs=(
            P("expert", "hidden"),
            P("expert", None),
            P("expert", None, "hidden"),
            P("expert", None, "hidden"),
            P("expert", "hidden", None),
        ),
        check_vma=False,
    )
```

```python
import jax
import jax.numpy as jnp
from jax import lax
from jax.experimental import pallas as pl
from jax.experimental.pallas import tpu as pltpu
from jax.sharding import PartitionSpec as P

D = 2048
SCALE = D ** (-0.5)
OWN = 32
NZ = 4
LOC = 4
CAP = 8
TOK = 256
QF = D // NZ
QH = 256
RA = 384
RB = QF - RA
WR = NZ * RB + 128
BF = jnp.bfloat16
F32 = jnp.float32
MIB = 1024 * 1024
ROUTE = 56
LAST = 56


def dot(a, b, ca, cb):
    return lax.dot_general(a, b, (((ca,), (cb,)), ((), ())), preferred_element_type=F32)


def shift(x, d):
    return lax.ppermute(x, "hidden", [(i, (i + d) % NZ) for i in range(NZ)])


def params(mib=63):
    return pltpu.CompilerParams(vmem_limit_bytes=mib * MIB)


def slots_of(dest, base, rows):
    slot = lax.broadcasted_iota(jnp.int32, (rows, TOK), 0) + base
    return slot == dest[0:1, :], slot == dest[1:2, :]


def route_first(zones, tokens, pay, dest_out, dest):
    step = pl.program_id(0)

    @pl.when(step == 0)
    def _():
        expert = lax.broadcasted_iota(jnp.int32, (OWN * LOC, TOK), 0)
        hit0 = expert == zones[0:1, :]
        hit1 = expert == zones[1:2, :]
        both = jnp.where(hit0 | hit1, 1.0, 0.0).astype(BF)
        earlier = lax.broadcasted_iota(jnp.int32, (TOK, TOK), 0) < lax.broadcasted_iota(
            jnp.int32, (TOK, TOK), 1
        )
        count = dot(both, jnp.where(earlier, 1.0, 0.0).astype(BF), 1, 0)
        rank0 = jnp.sum(jnp.where(hit0, count, 0.0), axis=0, keepdims=True)
        rank1 = jnp.sum(jnp.where(hit1, count, 0.0), axis=0, keepdims=True)
        dest[0:1, :] = zones[0:1, :] * CAP + rank0.astype(jnp.int32)
        dest[1:2, :] = zones[1:2, :] * CAP + rank1.astype(jnp.int32)
        dest_out[...] = dest[...]

    at0, at1 = slots_of(dest, step * 256, 256)
    pick = jnp.where(at0 | at1, 1.0, 0.0).astype(BF)
    pay[...] = dot(pick, tokens[...], 1, 0).astype(BF).reshape(8, 32, QF)


def picked(dest, weights):
    at0, at1 = slots_of(dest, pl.program_id(0) * 256, 256)
    pick = jnp.where(at0 | at1, 1.0, 0.0).astype(BF)
    w = jnp.sum(
        jnp.where(at0, weights[0:1, :], 0.0) + jnp.where(at1, weights[1:2, :], 0.0),
        axis=1,
        keepdims=True,
    )
    return pick, w


def route_rest(z_ref, dest, weights, c0, c1, c2, c3, pay):
    pick, w = picked(dest, weights)
    for off, c in enumerate((c0, c1, c2, c3)):
        dy = (dot(pick, c[...], 1, 0) * w).astype(BF)
        q = lax.rem(z_ref[0] + off, NZ)
        pay[:, :, pl.ds(pl.multiple_of(q * QF, QF), QF)] = dy.reshape(8, 32, QF)


def merged(v):
    n, r, f = v.shape
    return v.astype(F32).reshape(n * r, f).astype(BF)


def parted(v):
    return v.reshape(v.shape[0] // CAP, CAP, v.shape[1]).astype(BF)


def gates(
    z_ref, dest, own, left_a, left_b, right_a, right_b, far_a, far_b, wg, wu,
    x_out, h_out, silu_out, slope_out, pick_out, xs,
):
    at0, at1 = slots_of(dest, pl.program_id(0) * 256, 256)
    pick_out[...] = jnp.where(at0 | at1, 1.0, 0.0).T.astype(BF)
    pieces = ((0, (own,)), (3, (left_a, left_b)), (1, (right_a, right_b)), (2, (far_a, far_b)))
    for off, parts in pieces:
        q = lax.rem(z_ref[0] + off, NZ)
        row = 0
        for part in parts:
            n = part.shape[0] * CAP
            xs[q, row : row + n, :] = merged(part[:, 0])
            row += n
    g = u = 0.0
    for q in range(NZ):
        rows = slice(q * QF, (q + 1) * QF)
        x_out[0, :, rows] = xs[q]
        g = g + dot(xs[q], wg[0, rows, :], 1, 0)
        u = u + dot(xs[q], wu[0, rows, :], 1, 0)
    sig = jax.nn.sigmoid(g)
    silu = g * sig
    h_out[0] = (silu * u).astype(BF)
    silu_out[0] = silu
    slope_out[0] = u * sig * (1.0 + g * (1.0 - sig))


def middle(
    z_ref, rest, h_in, silu, slope, wg, wu, wd,
    o0t, o0b, o1t, o1b, o2t, o2b, o3t, o3b, part_out, dg_out, du_out,
):
    z = z_ref[0]
    h = h_in[0]
    dh = dot(merged(rest[:, 0]), wd[0], 1, 1)
    dg = (dh * slope[0]).astype(BF)
    du = (dh * silu[0]).astype(BF)
    dg_out[0] = dg
    du_out[0] = du
    mix = jnp.sum(h.astype(F32) * dh, axis=1, keepdims=True)
    high = mix.astype(BF).astype(F32)
    lane = lax.broadcasted_iota(jnp.int32, (OWN * CAP, 128), 1)
    mix = jnp.where(lane == 0, high, jnp.where(lane == 1, mix - high, 0.0))
    part_out[:, 0, :, NZ * RB :] = parted(mix)
    half = OWN * CAP // 2
    for off, top, bot in ((2, o2t, o2b), (1, o1t, o1b), (3, o3t, o3b), (0, o0t, o0b)):
        rows = pl.ds(pl.multiple_of(lax.rem(z + off, NZ) * QF, QF), QF)
        dx = dot(dg, wg[0, rows, :], 1, 1) + dot(du, wu[0, rows, :], 1, 1)
        top[:, 0] = parted(dx[:half, :RA])
        bot[:, 0] = parted(dx[half:, :RA])
        part_out[:, 0, :, off * RB : (off + 1) * RB] = parted(dx[:, RA:])


def last_sums(a0, a1, a2, b0, b1, b2, out):
    out[0] = (a0[...].astype(F32) + a1[...].astype(F32) + a2[...].astype(F32)).astype(BF)
    out[1] = (b0[...].astype(F32) + b1[...].astype(F32) + b2[...].astype(F32)).astype(BF)


def grads_down(rest, h, down_out):
    down_out[0] = dot(h[0], merged(rest[:, 0]), 0, 0).astype(BF)


def grads_up(x, dg, du, gate_out, up_out):
    gate_out[0] = dot(x[0], dg[0], 0, 0).astype(BF)
    up_out[0] = dot(x[0], du[0], 0, 0).astype(BF)


def pick_pairs(dest, back, y0, y1, y2, y3, ys):
    at0, at1 = slots_of(dest, 0, OWN * LOC * CAP)
    one0 = jnp.where(at0, 1.0, 0.0).astype(BF)
    one1 = jnp.where(at1, 1.0, 0.0).astype(BF)
    ys[...] = dot(one0 + one1, back[:, : NZ * RB], 0, 0)
    m0 = dot(back[:, NZ * RB :], one0, 0, 0)
    m1 = dot(back[:, NZ * RB :], one1, 0, 0)
    rows = [m[:8, c : c + RB] for m in (m0, m1) for c in range(0, TOK, RB)]
    mix = jnp.concatenate(rows, axis=0).astype(BF)
    for off, out in enumerate((y0, y1, y2, y3)):
        out[:TOK, :] = ys[:, off * RB : (off + 1) * RB].astype(BF)
        out[TOK:, :] = mix


def finish(pick, weights, back, y0, y1, y2, y3, grad_out, mix_out):
    grad_out[:, :RA] = dot(pick[...], back[...], 1, 0).astype(BF)
    y = (y0[...].astype(F32) + y2[...].astype(F32)) + (y1[...].astype(F32) + y3[...].astype(F32))
    grad_out[:, RA:] = y[:TOK].astype(BF)
    for k in range(2):
        for c in range(2):
            row = TOK + 8 * (2 * k + c)
            lanes = slice(c * RB, (c + 1) * RB)
            total = y[row : row + 1] + y[row + 1 : row + 2]
            mix_out[k : k + 1, lanes] = total * SCALE / weights[k : k + 1, lanes]


def shape(dims, dtype=BF):
    return pltpu.HBM(dims, dtype)


def cost(flops, size):
    return pl.CostEstimate(flops=int(flops), bytes_accessed=int(size), transcendentals=0)


def whole(dims):
    return pl.BlockSpec(dims, lambda i: (0,) * len(dims))


def by_expert(n, width):
    return pl.BlockSpec((n, 1, CAP, width), lambda e: (0, e, 0, 0))


def leading(*dims):
    return pl.BlockSpec((1,) + dims, lambda e: (e,) + (0,) * len(dims))


def on_device(tokens, cotangent, zone_ids, gate_weights, gate_proj, up_proj, down_proj):
    z = lax.axis_index("hidden").astype(jnp.int32).reshape(1)
    zones, weights = zone_ids.T, gate_weights.T
    smem = pl.BlockSpec(memory_space=pltpu.SMEM)
    pay, dest = pl.pallas_call(
        route_first,
        grid=(4,),
        in_specs=[whole((2, TOK)), whole((TOK, QF))],
        out_specs=[pl.BlockSpec((8, 32, QF), lambda i: (i, 0, 0)), whole((2, TOK))],
        out_shape=[shape((OWN, 32, QF)), shape((2, TOK), jnp.int32)],
        scratch_shapes=[pltpu.VMEM((2, TOK), jnp.int32)],
        compiler_params=params(),
        cost_estimate=cost(5e8, 4e6),
        name="route_first",
    )(zones, tokens)
    got = lax.all_to_all(pay, "expert", split_axis=0, concat_axis=0, tiled=True)

    c1, c2, c3 = shift(cotangent, -1), shift(cotangent, 2), shift(cotangent, 1)
    c1, c2, c3 = (pltpu.with_memory_space_constraint(c, pltpu.VMEM) for c in (c1, c2, c3))
    pay_rest = pl.pallas_call(
        route_rest,
        grid=(4,),
        in_specs=[smem, whole((2, TOK)), whole((2, TOK))] + [whole((TOK, QF))] * 4,
        out_specs=pl.BlockSpec((8, 32, D), lambda i: (i, 0, 0)),
        out_shape=shape((OWN, 32, D)),
        compiler_params=params(ROUTE),
        cost_estimate=cost(8e8, 6e6),
        name="route_rest",
    )(z, dest, weights, cotangent, c1, c2, c3)
    rest = lax.all_to_all(pay_rest, "expert", split_axis=0, concat_axis=0, tiled=True)
    rest = rest.reshape(OWN, LOC, CAP, D)

    half = OWN // 2
    got = got.reshape(OWN, LOC, CAP, QF)
    top, bot = got[:half], got[half:]
    left_t = shift(top, 1)
    right_b = shift(bot, -1)
    left_b = shift(bot, 1)
    right_t = shift(top, -1)
    far_t = shift(left_t, 1)
    far_b = shift(right_b, -1)

    left_b, right_t, far_t, far_b = (
        pltpu.with_memory_space_constraint(v, pltpu.VMEM) for v in (left_b, right_t, far_t, far_b)
    )
    rows = OWN * CAP
    hid, hid_f = shape((LOC, rows, QH)), shape((LOC, rows, QH), F32)
    hid_spec = leading(rows, QH)
    x_slots, h, silu, slope, pick = pl.pallas_call(
        gates,
        grid=(LOC,),
        in_specs=[smem, whole((2, TOK)), by_expert(OWN, QF)]
        + [by_expert(half, QF)] * 6 + [leading(D, QH)] * 2,
        out_specs=[leading(rows, D), hid_spec, hid_spec, hid_spec]
        + [pl.BlockSpec((TOK, 256), lambda e: (0, e))],
        out_shape=[shape((LOC, rows, D)), hid, hid_f, hid_f, shape((TOK, OWN * LOC * CAP))],
        scratch_shapes=[pltpu.VMEM((NZ, rows, QF), BF)],
        compiler_params=params(56),
        cost_estimate=cost(2.2e9, 19e6),
        name="gates",
    )(z, dest, got, left_t, left_b, right_t, right_b, far_t, far_b, gate_proj, up_proj)

    half_part = shape((half, LOC, CAP, RA))
    o0t, o0b, o1t, o1b, o2t, o2b, o3t, o3b, part, dg, du = pl.pallas_call(
        middle,
        grid=(LOC,),
        in_specs=[smem, by_expert(OWN, D)] + [hid_spec] * 3
        + [leading(D, QH), leading(D, QH), leading(QH, D)],
        out_specs=[by_expert(half, RA)] * 8 + [by_expert(OWN, WR)] + [hid_spec] * 2,
        out_shape=[half_part] * 8 + [shape((OWN, LOC, CAP, WR)), hid, hid],
        compiler_params=params(),
        cost_estimate=cost(2.7e9, 27e6),
        name="middle",
    )(z, rest, h, silu, slope, gate_proj, up_proj, down_proj)

    relay_t = shift(o2t, 1)
    relay_b = shift(o2b, -1)
    from_l_b = shift(o1b, 1)
    from_r_t = shift(o3t, -1)

    part_back = lax.all_to_all(
        part.reshape(OWN, 32, WR), "expert", split_axis=0, concat_axis=0, tiled=True
    ).reshape(OWN * 32, WR)


    sum_t = (o1t.astype(F32) + relay_t.astype(F32)).astype(BF)
    sum_b = (o3b.astype(F32) + relay_b.astype(F32)).astype(BF)
    from_l_t = shift(sum_t, 1)
    from_r_b = shift(sum_b, -1)

    sum_t, sum_b, dg, du = lax.optimization_barrier((sum_t, sum_b, dg, du))
    gate_grad, up_grad = pl.pallas_call(
        grads_up,
        grid=(LOC,),
        in_specs=[leading(rows, D)] + [hid_spec] * 2,
        out_specs=[leading(D, QH), leading(D, QH)],
        out_shape=[shape((LOC, D, QH)), shape((LOC, D, QH))],
        compiler_params=params(56),
        cost_estimate=cost(1.2e10, 20e6),
        name="grads_up",
    )(x_slots, dg, du)
    from_l_b, from_r_t, up_grad = lax.optimization_barrier((from_l_b, from_r_t, up_grad))
    terms = (o0t, from_l_t, from_r_t, o0b, from_l_b, from_r_b)
    sums = pl.pallas_call(
        last_sums,
        in_specs=[pl.BlockSpec(memory_space=pltpu.VMEM)] * 6,
        out_specs=pl.BlockSpec(memory_space=pltpu.VMEM),
        out_shape=jax.ShapeDtypeStruct((2, half, LOC, CAP, RA), BF),
        compiler_params=params(56),
        cost_estimate=cost(2e6, 3.2e6),
        name="last_sums",
    )(*(pltpu.with_memory_space_constraint(v, pltpu.VMEM) for v in terms))
    sums, h = lax.optimization_barrier((sums, h))
    down_grad = pl.pallas_call(
        grads_down,
        grid=(LOC,),
        in_specs=[by_expert(OWN, D), hid_spec],
        out_specs=leading(QH, D),
        out_shape=shape((LOC, QH, D)),
        compiler_params=params(),
        cost_estimate=cost(1.1e9, 10e6),
        name="grads_down",
    )(rest, h)
    back = lax.all_to_all(
        sums.reshape(OWN, 32, RA), "expert", split_axis=0, concat_axis=0, tiled=True
    ).reshape(OWN * 32, RA)

    y_shape = shape((TOK + 32, RB))
    y0, y1, y2, y3 = pl.pallas_call(
        pick_pairs,
        in_specs=[pl.BlockSpec(memory_space=pltpu.VMEM)] * 2,
        out_shape=[y_shape] * 4,
        scratch_shapes=[pltpu.VMEM((TOK, NZ * RB), F32)],
        compiler_params=params(56),
        cost_estimate=cost(4e8, 3e6),
        name="pick_pairs",
    )(dest, pltpu.with_memory_space_constraint(part_back, pltpu.VMEM))
    ys = (y0, shift(y1, 1), shift(y2, 2), shift(y3, -1))

    back = pltpu.with_memory_space_constraint(back, pltpu.VMEM)
    input_grad, mix_t = pl.pallas_call(
        finish,
        out_specs=[pl.BlockSpec(memory_space=pltpu.VMEM)] * 2,
        out_shape=[jax.ShapeDtypeStruct((TOK, QF), BF), jax.ShapeDtypeStruct((2, TOK), F32)],
        compiler_params=params(LAST),
        cost_estimate=cost(4e8, 3e6),
        name="finish",
    )(pick, weights, back, *ys)
    return (input_grad, mix_t.T, gate_grad, up_grad, down_grad)


def solution(mesh):
    return jax.shard_map(
        on_device,
        mesh=mesh,
        in_specs=(
            P("expert", "hidden"),
            P("expert", "hidden"),
            P("expert", None),
            P("expert", None),
            P("expert", None, "hidden"),
            P("expert", None, "hidden"),
            P("expert", "hidden", None),
        ),
        out_specs=(
            P("expert", "hidden"),
            P("expert", None),
            P("expert", None, "hidden"),
            P("expert", None, "hidden"),
            P("expert", "hidden", None),
        ),
        check_vma=False,
    )
```

```python
import jax
import jax.numpy as jnp
from jax import lax
from jax.experimental import pallas as pl
from jax.experimental.pallas import tpu as pltpu
from jax.sharding import PartitionSpec as P

D = 2048
SCALE = D ** (-0.5)
OWN = 32
NZ = 4
LOC = 4
CAP = 8
TOK = 256
QF = D // NZ
QH = 256
RA = 384
RB = QF - RA
WR = NZ * RB + 128
BF = jnp.bfloat16
F32 = jnp.float32
MIB = 1024 * 1024
ROUTE = 56
LAST = 56


def dot(a, b, ca, cb):
    return lax.dot_general(a, b, (((ca,), (cb,)), ((), ())), preferred_element_type=F32)


def shift(x, d):
    return lax.ppermute(x, "hidden", [(i, (i + d) % NZ) for i in range(NZ)])


def params(mib=63):
    return pltpu.CompilerParams(vmem_limit_bytes=mib * MIB)


def slots_of(dest, base, rows):
    slot = lax.broadcasted_iota(jnp.int32, (rows, TOK), 0) + base
    return slot == dest[0:1, :], slot == dest[1:2, :]


def route_first(zones, tokens, pay, dest_out, dest):
    step = pl.program_id(0)

    @pl.when(step == 0)
    def _():
        expert = lax.broadcasted_iota(jnp.int32, (OWN * LOC, TOK), 0)
        hit0 = expert == zones[0:1, :]
        hit1 = expert == zones[1:2, :]
        both = jnp.where(hit0 | hit1, 1.0, 0.0).astype(BF)
        earlier = lax.broadcasted_iota(jnp.int32, (TOK, TOK), 0) < lax.broadcasted_iota(
            jnp.int32, (TOK, TOK), 1
        )
        count = dot(both, jnp.where(earlier, 1.0, 0.0).astype(BF), 1, 0)
        rank0 = jnp.sum(jnp.where(hit0, count, 0.0), axis=0, keepdims=True)
        rank1 = jnp.sum(jnp.where(hit1, count, 0.0), axis=0, keepdims=True)
        dest[0:1, :] = zones[0:1, :] * CAP + rank0.astype(jnp.int32)
        dest[1:2, :] = zones[1:2, :] * CAP + rank1.astype(jnp.int32)
        dest_out[...] = dest[...]

    at0, at1 = slots_of(dest, step * 256, 256)
    pick = jnp.where(at0 | at1, 1.0, 0.0).astype(BF)
    pay[...] = dot(pick, tokens[...], 1, 0).astype(BF).reshape(8, 32, QF)


def picked(dest, weights):
    at0, at1 = slots_of(dest, pl.program_id(0) * 256, 256)
    pick = jnp.where(at0 | at1, 1.0, 0.0).astype(BF)
    w = jnp.sum(
        jnp.where(at0, weights[0:1, :], 0.0) + jnp.where(at1, weights[1:2, :], 0.0),
        axis=1,
        keepdims=True,
    )
    return pick, w


def route_rest(z_ref, dest, weights, c0, c1, c2, c3, pay):
    pick, w = picked(dest, weights)
    for off, c in enumerate((c0, c1, c2, c3)):
        dy = (dot(pick, c[...], 1, 0) * w).astype(BF)
        q = lax.rem(z_ref[0] + off, NZ)
        pay[:, :, pl.ds(pl.multiple_of(q * QF, QF), QF)] = dy.reshape(8, 32, QF)


def merged(v):
    n, r, f = v.shape
    return v.astype(F32).reshape(n * r, f).astype(BF)


def parted(v):
    return v.reshape(v.shape[0] // CAP, CAP, v.shape[1]).astype(BF)


def gates(
    z_ref, dest, own, left_a, left_b, right_a, right_b, far_a, far_b, wg, wu,
    x_out, h_out, silu_out, slope_out, pick_out, xs,
):
    at0, at1 = slots_of(dest, pl.program_id(0) * 256, 256)
    pick_out[...] = jnp.where(at0 | at1, 1.0, 0.0).T.astype(BF)
    pieces = ((0, (own,)), (3, (left_a, left_b)), (1, (right_a, right_b)), (2, (far_a, far_b)))
    for off, parts in pieces:
        q = lax.rem(z_ref[0] + off, NZ)
        row = 0
        for part in parts:
            n = part.shape[0] * CAP
            xs[q, row : row + n, :] = merged(part[:, 0])
            row += n
    g = u = 0.0
    for q in range(NZ):
        rows = slice(q * QF, (q + 1) * QF)
        x_out[0, :, rows] = xs[q]
        g = g + dot(xs[q], wg[0, rows, :], 1, 0)
        u = u + dot(xs[q], wu[0, rows, :], 1, 0)
    sig = jax.nn.sigmoid(g)
    silu = g * sig
    h_out[0] = (silu * u).astype(BF)
    silu_out[0] = silu
    slope_out[0] = u * sig * (1.0 + g * (1.0 - sig))


def middle(
    z_ref, rest, h_in, silu, slope, wg, wu, wd,
    o0t, o0b, o1t, o1b, o2t, o2b, o3t, o3b, part_out, dg_out, du_out,
):
    z = z_ref[0]
    h = h_in[0]
    dh = dot(merged(rest[:, 0]), wd[0], 1, 1)
    dg = (dh * slope[0]).astype(BF)
    du = (dh * silu[0]).astype(BF)
    dg_out[0] = dg
    du_out[0] = du
    mix = jnp.sum(h.astype(F32) * dh, axis=1, keepdims=True)
    high = mix.astype(BF).astype(F32)
    lane = lax.broadcasted_iota(jnp.int32, (OWN * CAP, 128), 1)
    mix = jnp.where(lane == 0, high, jnp.where(lane == 1, mix - high, 0.0))
    part_out[:, 0, :, NZ * RB :] = parted(mix)
    half = OWN * CAP // 2
    for off, top, bot in ((2, o2t, o2b), (1, o1t, o1b), (3, o3t, o3b), (0, o0t, o0b)):
        rows = pl.ds(pl.multiple_of(lax.rem(z + off, NZ) * QF, QF), QF)
        dx = dot(dg, wg[0, rows, :], 1, 1) + dot(du, wu[0, rows, :], 1, 1)
        top[:, 0] = parted(dx[:half, :RA])
        bot[:, 0] = parted(dx[half:, :RA])
        part_out[:, 0, :, off * RB : (off + 1) * RB] = parted(dx[:, RA:])


def last_sums(a0, a1, a2, b0, b1, b2, out):
    out[0] = (a0[...].astype(F32) + a1[...].astype(F32) + a2[...].astype(F32)).astype(BF)
    out[1] = (b0[...].astype(F32) + b1[...].astype(F32) + b2[...].astype(F32)).astype(BF)


def grads_down(rest, h, down_out):
    down_out[0] = dot(h[0], merged(rest[:, 0]), 0, 0).astype(BF)


def grads_up(x, dg, du, gate_out, up_out):
    gate_out[0] = dot(x[0], dg[0], 0, 0).astype(BF)
    up_out[0] = dot(x[0], du[0], 0, 0).astype(BF)


def pick_pairs(dest, back, y0, y1, y2, y3, ys):
    at0, at1 = slots_of(dest, 0, OWN * LOC * CAP)
    one0 = jnp.where(at0, 1.0, 0.0).astype(BF)
    one1 = jnp.where(at1, 1.0, 0.0).astype(BF)
    ys[...] = dot(one0 + one1, back[:, : NZ * RB], 0, 0)
    m0 = dot(back[:, NZ * RB :], one0, 0, 0)
    m1 = dot(back[:, NZ * RB :], one1, 0, 0)
    rows = [m[:8, c : c + RB] for m in (m0, m1) for c in range(0, TOK, RB)]
    mix = jnp.concatenate(rows, axis=0).astype(BF)
    for off, out in enumerate((y0, y1, y2, y3)):
        out[:TOK, :] = ys[:, off * RB : (off + 1) * RB].astype(BF)
        out[TOK:, :] = mix


def finish(pick, weights, back, y0, y1, y2, y3, grad_out, mix_out):
    grad_out[:, :RA] = dot(pick[...], back[...], 1, 0).astype(BF)
    y = (y0[...].astype(F32) + y2[...].astype(F32)) + (y1[...].astype(F32) + y3[...].astype(F32))
    grad_out[:, RA:] = y[:TOK].astype(BF)
    for k in range(2):
        for c in range(2):
            row = TOK + 8 * (2 * k + c)
            lanes = slice(c * RB, (c + 1) * RB)
            total = y[row : row + 1] + y[row + 1 : row + 2]
            mix_out[k : k + 1, lanes] = total * SCALE / weights[k : k + 1, lanes]


def shape(dims, dtype=BF):
    return pltpu.HBM(dims, dtype)


def cost(flops, size):
    return pl.CostEstimate(flops=int(flops), bytes_accessed=int(size), transcendentals=0)


def whole(dims):
    return pl.BlockSpec(dims, lambda i: (0,) * len(dims))


def by_expert(n, width):
    return pl.BlockSpec((n, 1, CAP, width), lambda e: (0, e, 0, 0))


def leading(*dims):
    return pl.BlockSpec((1,) + dims, lambda e: (e,) + (0,) * len(dims))


def on_device(tokens, cotangent, zone_ids, gate_weights, gate_proj, up_proj, down_proj):
    z = lax.axis_index("hidden").astype(jnp.int32).reshape(1)
    zones, weights = zone_ids.T, gate_weights.T
    smem = pl.BlockSpec(memory_space=pltpu.SMEM)
    pay, dest = pl.pallas_call(
        route_first,
        grid=(4,),
        in_specs=[whole((2, TOK)), whole((TOK, QF))],
        out_specs=[pl.BlockSpec((8, 32, QF), lambda i: (i, 0, 0)), whole((2, TOK))],
        out_shape=[shape((OWN, 32, QF)), shape((2, TOK), jnp.int32)],
        scratch_shapes=[pltpu.VMEM((2, TOK), jnp.int32)],
        compiler_params=params(),
        cost_estimate=cost(5e8, 4e6),
        name="route_first",
    )(zones, tokens)
    got = lax.all_to_all(pay, "expert", split_axis=0, concat_axis=0, tiled=True)

    c1, c2, c3 = shift(cotangent, -1), shift(cotangent, 2), shift(cotangent, 1)
    c1, c2, c3 = (pltpu.with_memory_space_constraint(c, pltpu.VMEM) for c in (c1, c2, c3))
    pay_rest = pl.pallas_call(
        route_rest,
        grid=(4,),
        in_specs=[smem, whole((2, TOK)), whole((2, TOK))] + [whole((TOK, QF))] * 4,
        out_specs=pl.BlockSpec((8, 32, D), lambda i: (i, 0, 0)),
        out_shape=shape((OWN, 32, D)),
        compiler_params=params(ROUTE),
        cost_estimate=cost(8e8, 6e6),
        name="route_rest",
    )(z, dest, weights, cotangent, c1, c2, c3)
    rest = lax.all_to_all(pay_rest, "expert", split_axis=0, concat_axis=0, tiled=True)
    rest = rest.reshape(OWN, LOC, CAP, D)

    half = OWN // 2
    got = got.reshape(OWN, LOC, CAP, QF)
    top, bot = got[:half], got[half:]
    left_t = shift(top, 1)
    right_b = shift(bot, -1)
    left_b = shift(bot, 1)
    right_t = shift(top, -1)
    far_t = shift(left_t, 1)
    far_b = shift(right_b, -1)

    left_b, right_t, far_t, far_b = (
        pltpu.with_memory_space_constraint(v, pltpu.VMEM) for v in (left_b, right_t, far_t, far_b)
    )
    rows = OWN * CAP
    hid, hid_f = shape((LOC, rows, QH)), shape((LOC, rows, QH), F32)
    hid_spec = leading(rows, QH)
    x_slots, h, silu, slope, pick = pl.pallas_call(
        gates,
        grid=(LOC,),
        in_specs=[smem, whole((2, TOK)), by_expert(OWN, QF)]
        + [by_expert(half, QF)] * 6 + [leading(D, QH)] * 2,
        out_specs=[leading(rows, D), hid_spec, hid_spec, hid_spec]
        + [pl.BlockSpec((TOK, 256), lambda e: (0, e))],
        out_shape=[shape((LOC, rows, D)), hid, hid_f, hid_f, shape((TOK, OWN * LOC * CAP))],
        scratch_shapes=[pltpu.VMEM((NZ, rows, QF), BF)],
        compiler_params=params(56),
        cost_estimate=cost(2.2e9, 19e6),
        name="gates",
    )(z, dest, got, left_t, left_b, right_t, right_b, far_t, far_b, gate_proj, up_proj)

    half_part = shape((half, LOC, CAP, RA))
    o0t, o0b, o1t, o1b, o2t, o2b, o3t, o3b, part, dg, du = pl.pallas_call(
        middle,
        grid=(LOC,),
        in_specs=[smem, by_expert(OWN, D)] + [hid_spec] * 3
        + [leading(D, QH), leading(D, QH), leading(QH, D)],
        out_specs=[by_expert(half, RA)] * 8 + [by_expert(OWN, WR)] + [hid_spec] * 2,
        out_shape=[half_part] * 8 + [shape((OWN, LOC, CAP, WR)), hid, hid],
        compiler_params=params(),
        cost_estimate=cost(2.7e9, 27e6),
        name="middle",
    )(z, rest, h, silu, slope, gate_proj, up_proj, down_proj)

    relay_t = shift(o2t, 1)
    relay_b = shift(o2b, -1)
    from_l_b = shift(o1b, 1)
    from_r_t = shift(o3t, -1)

    part_back = lax.all_to_all(
        part.reshape(OWN, 32, WR), "expert", split_axis=0, concat_axis=0, tiled=True
    ).reshape(OWN * 32, WR)


    sum_t = (o1t.astype(F32) + relay_t.astype(F32)).astype(BF)
    sum_b = (o3b.astype(F32) + relay_b.astype(F32)).astype(BF)
    from_l_t = shift(sum_t, 1)
    from_r_b = shift(sum_b, -1)

    sum_t, sum_b, dg, du = lax.optimization_barrier((sum_t, sum_b, dg, du))
    gate_grad, up_grad = pl.pallas_call(
        grads_up,
        grid=(LOC,),
        in_specs=[leading(rows, D)] + [hid_spec] * 2,
        out_specs=[leading(D, QH), leading(D, QH)],
        out_shape=[shape((LOC, D, QH)), shape((LOC, D, QH))],
        compiler_params=params(56),
        cost_estimate=cost(1.2e10, 20e6),
        name="grads_up",
    )(x_slots, dg, du)
    from_l_b, from_r_t, up_grad = lax.optimization_barrier((from_l_b, from_r_t, up_grad))
    terms = (o0t, from_l_t, from_r_t, o0b, from_l_b, from_r_b)
    sums = pl.pallas_call(
        last_sums,
        in_specs=[pl.BlockSpec(memory_space=pltpu.VMEM)] * 6,
        out_specs=pl.BlockSpec(memory_space=pltpu.VMEM),
        out_shape=jax.ShapeDtypeStruct((2, half, LOC, CAP, RA), BF),
        compiler_params=params(56),
        cost_estimate=cost(2e6, 3.2e6),
        name="last_sums",
    )(*(pltpu.with_memory_space_constraint(v, pltpu.VMEM) for v in terms))
    sums, h = lax.optimization_barrier((sums, h))
    down_grad = pl.pallas_call(
        grads_down,
        grid=(LOC,),
        in_specs=[by_expert(OWN, D), hid_spec],
        out_specs=leading(QH, D),
        out_shape=shape((LOC, QH, D)),
        compiler_params=params(56),
        cost_estimate=cost(1.1e9, 10e6),
        name="grads_down",
    )(rest, h)
    back = lax.all_to_all(
        sums.reshape(OWN, 32, RA), "expert", split_axis=0, concat_axis=0, tiled=True
    ).reshape(OWN * 32, RA)

    y_shape = shape((TOK + 32, RB))
    y0, y1, y2, y3 = pl.pallas_call(
        pick_pairs,
        in_specs=[pl.BlockSpec(memory_space=pltpu.VMEM)] * 2,
        out_shape=[y_shape] * 4,
        scratch_shapes=[pltpu.VMEM((TOK, NZ * RB), F32)],
        compiler_params=params(56),
        cost_estimate=cost(4e8, 3e6),
        name="pick_pairs",
    )(dest, pltpu.with_memory_space_constraint(part_back, pltpu.VMEM))
    ys = (y0, shift(y1, 1), shift(y2, 2), shift(y3, -1))

    pick, back, *ys = (
        pltpu.with_memory_space_constraint(v, pltpu.VMEM) for v in (pick, back, *ys)
    )
    input_grad, mix_t = pl.pallas_call(
        finish,
        out_specs=[pl.BlockSpec(memory_space=pltpu.VMEM)] * 2,
        out_shape=[jax.ShapeDtypeStruct((TOK, QF), BF), jax.ShapeDtypeStruct((2, TOK), F32)],
        compiler_params=params(LAST),
        cost_estimate=cost(4e8, 3e6),
        name="finish",
    )(pick, weights, back, *ys)
    return (input_grad, mix_t.T, gate_grad, up_grad, down_grad)


def solution(mesh):
    return jax.shard_map(
        on_device,
        mesh=mesh,
        in_specs=(
            P("expert", "hidden"),
            P("expert", "hidden"),
            P("expert", None),
            P("expert", None),
            P("expert", None, "hidden"),
            P("expert", None, "hidden"),
            P("expert", "hidden", None),
        ),
        out_specs=(
            P("expert", "hidden"),
            P("expert", None),
            P("expert", None, "hidden"),
            P("expert", None, "hidden"),
            P("expert", "hidden", None),
        ),
        check_vma=False,
    )
```

```python
import jax
import jax.numpy as jnp
from jax import lax
from jax.experimental import pallas as pl
from jax.experimental.pallas import tpu as pltpu
from jax.sharding import PartitionSpec as P

D = 2048
SCALE = D ** (-0.5)
OWN = 32
NZ = 4
LOC = 4
CAP = 8
TOK = 256
QF = D // NZ
QH = 256
RA = 384
RB = QF - RA
WR = NZ * RB + 128
BF = jnp.bfloat16
F32 = jnp.float32
MIB = 1024 * 1024
ROUTE = 56
LAST = 56


def dot(a, b, ca, cb):
    return lax.dot_general(a, b, (((ca,), (cb,)), ((), ())), preferred_element_type=F32)


def shift(x, d):
    return lax.ppermute(x, "hidden", [(i, (i + d) % NZ) for i in range(NZ)])


def params(mib=63):
    return pltpu.CompilerParams(vmem_limit_bytes=mib * MIB)


def slots_of(dest, base, rows):
    slot = lax.broadcasted_iota(jnp.int32, (rows, TOK), 0) + base
    return slot == dest[0:1, :], slot == dest[1:2, :]


def route_first(zones, tokens, pay, dest_out, dest):
    step = pl.program_id(0)

    @pl.when(step == 0)
    def _():
        expert = lax.broadcasted_iota(jnp.int32, (OWN * LOC, TOK), 0)
        hit0 = expert == zones[0:1, :]
        hit1 = expert == zones[1:2, :]
        both = jnp.where(hit0 | hit1, 1.0, 0.0).astype(BF)
        earlier = lax.broadcasted_iota(jnp.int32, (TOK, TOK), 0) < lax.broadcasted_iota(
            jnp.int32, (TOK, TOK), 1
        )
        count = dot(both, jnp.where(earlier, 1.0, 0.0).astype(BF), 1, 0)
        rank0 = jnp.sum(jnp.where(hit0, count, 0.0), axis=0, keepdims=True)
        rank1 = jnp.sum(jnp.where(hit1, count, 0.0), axis=0, keepdims=True)
        dest[0:1, :] = zones[0:1, :] * CAP + rank0.astype(jnp.int32)
        dest[1:2, :] = zones[1:2, :] * CAP + rank1.astype(jnp.int32)
        dest_out[...] = dest[...]

    at0, at1 = slots_of(dest, step * 256, 256)
    pick = jnp.where(at0 | at1, 1.0, 0.0).astype(BF)
    pay[...] = dot(pick, tokens[...], 1, 0).astype(BF).reshape(8, 32, QF)


def picked(dest, weights):
    at0, at1 = slots_of(dest, pl.program_id(0) * 256, 256)
    pick = jnp.where(at0 | at1, 1.0, 0.0).astype(BF)
    w = jnp.sum(
        jnp.where(at0, weights[0:1, :], 0.0) + jnp.where(at1, weights[1:2, :], 0.0),
        axis=1,
        keepdims=True,
    )
    return pick, w


def route_rest(z_ref, dest, weights, c0, c1, c2, c3, pay):
    pick, w = picked(dest, weights)
    for off, c in enumerate((c0, c1, c2, c3)):
        dy = (dot(pick, c[...], 1, 0) * w).astype(BF)
        q = lax.rem(z_ref[0] + off, NZ)
        pay[:, :, pl.ds(pl.multiple_of(q * QF, QF), QF)] = dy.reshape(8, 32, QF)


def merged(v):
    n, r, f = v.shape
    return v.astype(F32).reshape(n * r, f).astype(BF)


def parted(v):
    return v.reshape(v.shape[0] // CAP, CAP, v.shape[1]).astype(BF)


def gates(
    z_ref, dest, own, left_a, left_b, right_a, right_b, far_a, far_b, wg, wu,
    x_out, h_out, silu_out, slope_out, pick_out, xs,
):
    at0, at1 = slots_of(dest, pl.program_id(0) * 256, 256)
    pick_out[...] = jnp.where(at0 | at1, 1.0, 0.0).T.astype(BF)
    pieces = ((0, (own,)), (3, (left_a, left_b)), (1, (right_a, right_b)), (2, (far_a, far_b)))
    for off, parts in pieces:
        q = lax.rem(z_ref[0] + off, NZ)
        row = 0
        for part in parts:
            n = part.shape[0] * CAP
            xs[q, row : row + n, :] = merged(part[:, 0])
            row += n
    g = u = 0.0
    for q in range(NZ):
        rows = slice(q * QF, (q + 1) * QF)
        x_out[0, :, rows] = xs[q]
        g = g + dot(xs[q], wg[0, rows, :], 1, 0)
        u = u + dot(xs[q], wu[0, rows, :], 1, 0)
    sig = jax.nn.sigmoid(g)
    silu = g * sig
    h_out[0] = (silu * u).astype(BF)
    silu_out[0] = silu
    slope_out[0] = u * sig * (1.0 + g * (1.0 - sig))


def middle(
    z_ref, rest, h_in, silu, slope, wg, wu, wd,
    o0t, o0b, o1t, o1b, o2t, o2b, o3t, o3b, part_out, dg_out, du_out,
):
    z = z_ref[0]
    h = h_in[0]
    dh = dot(merged(rest[:, 0]), wd[0], 1, 1)
    dg = (dh * slope[0]).astype(BF)
    du = (dh * silu[0]).astype(BF)
    dg_out[0] = dg
    du_out[0] = du
    mix = jnp.sum(h.astype(F32) * dh, axis=1, keepdims=True)
    high = mix.astype(BF).astype(F32)
    lane = lax.broadcasted_iota(jnp.int32, (OWN * CAP, 128), 1)
    mix = jnp.where(lane == 0, high, jnp.where(lane == 1, mix - high, 0.0))
    part_out[:, 0, :, NZ * RB :] = parted(mix)
    half = OWN * CAP // 2
    for off, top, bot in ((2, o2t, o2b), (1, o1t, o1b), (3, o3t, o3b), (0, o0t, o0b)):
        rows = pl.ds(pl.multiple_of(lax.rem(z + off, NZ) * QF, QF), QF)
        dx = dot(dg, wg[0, rows, :], 1, 1) + dot(du, wu[0, rows, :], 1, 1)
        top[:, 0] = parted(dx[:half, :RA])
        bot[:, 0] = parted(dx[half:, :RA])
        part_out[:, 0, :, off * RB : (off + 1) * RB] = parted(dx[:, RA:])


def last_sums(a0, a1, a2, b0, b1, b2, out):
    out[0] = (a0[...].astype(F32) + a1[...].astype(F32) + a2[...].astype(F32)).astype(BF)
    out[1] = (b0[...].astype(F32) + b1[...].astype(F32) + b2[...].astype(F32)).astype(BF)


def grads_down(rest, h, down_out):
    down_out[0] = dot(h[0], merged(rest[:, 0]), 0, 0).astype(BF)


def grads_up(x, dg, du, gate_out, up_out):
    gate_out[0] = dot(x[0], dg[0], 0, 0).astype(BF)
    up_out[0] = dot(x[0], du[0], 0, 0).astype(BF)


def pick_pairs(dest, back, y0, y1, y2, y3, ys):
    at0, at1 = slots_of(dest, 0, OWN * LOC * CAP)
    one0 = jnp.where(at0, 1.0, 0.0).astype(BF)
    one1 = jnp.where(at1, 1.0, 0.0).astype(BF)
    ys[...] = dot(one0 + one1, back[:, : NZ * RB], 0, 0)
    m0 = dot(back[:, NZ * RB :], one0, 0, 0)
    m1 = dot(back[:, NZ * RB :], one1, 0, 0)
    rows = [m[:8, c : c + RB] for m in (m0, m1) for c in range(0, TOK, RB)]
    mix = jnp.concatenate(rows, axis=0).astype(BF)
    for off, out in enumerate((y0, y1, y2, y3)):
        out[:TOK, :] = ys[:, off * RB : (off + 1) * RB].astype(BF)
        out[TOK:, :] = mix


def finish(pick, weights, back, y0, y1, y2, y3, grad_out, mix_out):
    grad_out[:, :RA] = dot(pick[...], back[...], 1, 0).astype(BF)
    y = (y0[...].astype(F32) + y2[...].astype(F32)) + (y1[...].astype(F32) + y3[...].astype(F32))
    grad_out[:, RA:] = y[:TOK].astype(BF)
    for k in range(2):
        for c in range(2):
            row = TOK + 8 * (2 * k + c)
            lanes = slice(c * RB, (c + 1) * RB)
            total = y[row : row + 1] + y[row + 1 : row + 2]
            mix_out[k : k + 1, lanes] = total * SCALE / weights[k : k + 1, lanes]


def shape(dims, dtype=BF):
    return pltpu.HBM(dims, dtype)


def cost(flops, size):
    return pl.CostEstimate(flops=int(flops), bytes_accessed=int(size), transcendentals=0)


def whole(dims):
    return pl.BlockSpec(dims, lambda i: (0,) * len(dims))


def by_expert(n, width):
    return pl.BlockSpec((n, 1, CAP, width), lambda e: (0, e, 0, 0))


def leading(*dims):
    return pl.BlockSpec((1,) + dims, lambda e: (e,) + (0,) * len(dims))


def on_device(tokens, cotangent, zone_ids, gate_weights, gate_proj, up_proj, down_proj):
    z = lax.axis_index("hidden").astype(jnp.int32).reshape(1)
    zones, weights = zone_ids.T, gate_weights.T
    smem = pl.BlockSpec(memory_space=pltpu.SMEM)
    pay, dest = pl.pallas_call(
        route_first,
        grid=(4,),
        in_specs=[whole((2, TOK)), whole((TOK, QF))],
        out_specs=[pl.BlockSpec((8, 32, QF), lambda i: (i, 0, 0)), whole((2, TOK))],
        out_shape=[shape((OWN, 32, QF)), shape((2, TOK), jnp.int32)],
        scratch_shapes=[pltpu.VMEM((2, TOK), jnp.int32)],
        compiler_params=params(),
        cost_estimate=cost(5e8, 4e6),
        name="route_first",
    )(zones, tokens)
    got = lax.all_to_all(pay, "expert", split_axis=0, concat_axis=0, tiled=True)

    c1, c2, c3 = shift(cotangent, -1), shift(cotangent, 2), shift(cotangent, 1)
    c1, c2, c3 = (pltpu.with_memory_space_constraint(c, pltpu.VMEM) for c in (c1, c2, c3))
    pay_rest = pl.pallas_call(
        route_rest,
        grid=(4,),
        in_specs=[smem, whole((2, TOK)), whole((2, TOK))] + [whole((TOK, QF))] * 4,
        out_specs=pl.BlockSpec((8, 32, D), lambda i: (i, 0, 0)),
        out_shape=shape((OWN, 32, D)),
        compiler_params=params(ROUTE),
        cost_estimate=cost(8e8, 6e6),
        name="route_rest",
    )(z, dest, weights, cotangent, c1, c2, c3)
    rest = lax.all_to_all(pay_rest, "expert", split_axis=0, concat_axis=0, tiled=True)
    rest = rest.reshape(OWN, LOC, CAP, D)

    half = OWN // 2
    got = got.reshape(OWN, LOC, CAP, QF)
    top, bot = got[:half], got[half:]
    left_t = shift(top, 1)
    right_b = shift(bot, -1)
    left_b = shift(bot, 1)
    right_t = shift(top, -1)
    far_t = shift(left_t, 1)
    far_b = shift(right_b, -1)

    left_b, right_t, far_t, far_b = (
        pltpu.with_memory_space_constraint(v, pltpu.VMEM) for v in (left_b, right_t, far_t, far_b)
    )
    rows = OWN * CAP
    hid, hid_f = shape((LOC, rows, QH)), pltpu.VMEM((LOC, rows, QH), F32)
    hid_spec = leading(rows, QH)
    x_slots, h, silu, slope, pick = pl.pallas_call(
        gates,
        grid=(LOC,),
        in_specs=[smem, whole((2, TOK)), by_expert(OWN, QF)]
        + [by_expert(half, QF)] * 6 + [leading(D, QH)] * 2,
        out_specs=[leading(rows, D), hid_spec, hid_spec, hid_spec]
        + [pl.BlockSpec((TOK, 256), lambda e: (0, e))],
        out_shape=[shape((LOC, rows, D)), hid, hid_f, hid_f, shape((TOK, OWN * LOC * CAP))],
        scratch_shapes=[pltpu.VMEM((NZ, rows, QF), BF)],
        compiler_params=params(56),
        cost_estimate=cost(2.2e9, 19e6),
        name="gates",
    )(z, dest, got, left_t, left_b, right_t, right_b, far_t, far_b, gate_proj, up_proj)

    silu, slope = (pltpu.with_memory_space_constraint(v, pltpu.VMEM) for v in (silu, slope))
    half_part = shape((half, LOC, CAP, RA))
    o0t, o0b, o1t, o1b, o2t, o2b, o3t, o3b, part, dg, du = pl.pallas_call(
        middle,
        grid=(LOC,),
        in_specs=[smem, by_expert(OWN, D)] + [hid_spec] * 3
        + [leading(D, QH), leading(D, QH), leading(QH, D)],
        out_specs=[by_expert(half, RA)] * 8 + [by_expert(OWN, WR)] + [hid_spec] * 2,
        out_shape=[half_part] * 8 + [shape((OWN, LOC, CAP, WR)), hid, hid],
        compiler_params=params(58),
        cost_estimate=cost(2.7e9, 27e6),
        name="middle",
    )(z, rest, h, silu, slope, gate_proj, up_proj, down_proj)

    relay_t = shift(o2t, 1)
    relay_b = shift(o2b, -1)
    from_l_b = shift(o1b, 1)
    from_r_t = shift(o3t, -1)

    part_back = lax.all_to_all(
        part.reshape(OWN, 32, WR), "expert", split_axis=0, concat_axis=0, tiled=True
    ).reshape(OWN * 32, WR)


    sum_t = (o1t.astype(F32) + relay_t.astype(F32)).astype(BF)
    sum_b = (o3b.astype(F32) + relay_b.astype(F32)).astype(BF)
    from_l_t = shift(sum_t, 1)
    from_r_b = shift(sum_b, -1)

    sum_t, sum_b, dg, du = lax.optimization_barrier((sum_t, sum_b, dg, du))
    gate_grad, up_grad = pl.pallas_call(
        grads_up,
        grid=(LOC,),
        in_specs=[leading(rows, D)] + [hid_spec] * 2,
        out_specs=[leading(D, QH), leading(D, QH)],
        out_shape=[shape((LOC, D, QH)), shape((LOC, D, QH))],
        compiler_params=params(56),
        cost_estimate=cost(1.2e10, 20e6),
        name="grads_up",
    )(x_slots, dg, du)
    from_l_b, from_r_t, up_grad = lax.optimization_barrier((from_l_b, from_r_t, up_grad))
    terms = (o0t, from_l_t, from_r_t, o0b, from_l_b, from_r_b)
    sums = pl.pallas_call(
        last_sums,
        in_specs=[pl.BlockSpec(memory_space=pltpu.VMEM)] * 6,
        out_specs=pl.BlockSpec(memory_space=pltpu.VMEM),
        out_shape=jax.ShapeDtypeStruct((2, half, LOC, CAP, RA), BF),
        compiler_params=params(56),
        cost_estimate=cost(2e6, 3.2e6),
        name="last_sums",
    )(*(pltpu.with_memory_space_constraint(v, pltpu.VMEM) for v in terms))
    sums, h = lax.optimization_barrier((sums, h))
    down_grad = pl.pallas_call(
        grads_down,
        grid=(LOC,),
        in_specs=[by_expert(OWN, D), hid_spec],
        out_specs=leading(QH, D),
        out_shape=shape((LOC, QH, D)),
        compiler_params=params(56),
        cost_estimate=cost(1.1e9, 10e6),
        name="grads_down",
    )(rest, h)
    back = lax.all_to_all(
        sums.reshape(OWN, 32, RA), "expert", split_axis=0, concat_axis=0, tiled=True
    ).reshape(OWN * 32, RA)

    y_shape = shape((TOK + 32, RB))
    y0, y1, y2, y3 = pl.pallas_call(
        pick_pairs,
        in_specs=[pl.BlockSpec(memory_space=pltpu.VMEM)] * 2,
        out_shape=[y_shape] * 4,
        scratch_shapes=[pltpu.VMEM((TOK, NZ * RB), F32)],
        compiler_params=params(56),
        cost_estimate=cost(4e8, 3e6),
        name="pick_pairs",
    )(dest, pltpu.with_memory_space_constraint(part_back, pltpu.VMEM))
    ys = (y0, shift(y1, 1), shift(y2, 2), shift(y3, -1))

    pick, back, *ys = (
        pltpu.with_memory_space_constraint(v, pltpu.VMEM) for v in (pick, back, *ys)
    )
    input_grad, mix_t = pl.pallas_call(
        finish,
        out_specs=[pl.BlockSpec(memory_space=pltpu.VMEM)] * 2,
        out_shape=[jax.ShapeDtypeStruct((TOK, QF), BF), jax.ShapeDtypeStruct((2, TOK), F32)],
        compiler_params=params(LAST),
        cost_estimate=cost(4e8, 3e6),
        name="finish",
    )(pick, weights, back, *ys)
    return (input_grad, mix_t.T, gate_grad, up_grad, down_grad)


def solution(mesh):
    return jax.shard_map(
        on_device,
        mesh=mesh,
        in_specs=(
            P("expert", "hidden"),
            P("expert", "hidden"),
            P("expert", None),
            P("expert", None),
            P("expert", None, "hidden"),
            P("expert", None, "hidden"),
            P("expert", "hidden", None),
        ),
        out_specs=(
            P("expert", "hidden"),
            P("expert", None),
            P("expert", None, "hidden"),
            P("expert", None, "hidden"),
            P("expert", "hidden", None),
        ),
        check_vma=False,
    )
```
